512 devices in a mesh: blk: 32 (over z_lo, x), grp: 16 (over z_hi, y, core).
Axes of the slice: x: 4, y: 4, z: 16 (z_hi: 2, z_lo: 8; z = z_hi * 8 + z_lo), core: 2. Of those that a mesh axis runs over, the one named last changes fastest.
Arguments:
- positions: float32 [3, 32768], P(None, ('blk', 'grp')), may hold values from -0.25 to 31.25, as said below
- moments: float32 [2, 2, 3, 32768], P(None, None, None, ('blk', 'grp')), may hold values from -6 to 6
- inv_polar_re: float32 [32768], P(('blk', 'grp')), may hold values from 0.5 to 2
- inv_polar_im: float32 [32768], P(('blk', 'grp')), may hold values from -0.5 to 0.5
- mode_field: float32 [2, 3, 32768, 512], P(None, None, ('blk', 'grp')), may hold values from -0.0390625 to 0.0390625
- mode_detune: float32 [512], replicated, may hold values from -1 to 1
- mode_width: float32 [512], replicated, may hold values from 0.05 to 1
Outputs:
- response: float32 [2, 2, 3, 32768], P(None, None, None, ('blk', 'grp'))
The draws below stay inside these ranges and needn't reach their ends.
Inputs may be any that keep to these rules, and one draw needn't show every extreme that they name: `positions`: dipole n lies within 0.25, in each coordinate, of the lattice site (n % 32, (n // 32) % 32, n // 1024); distinct dipoles are at least 0.5 apart.
All inputs are finite; a program needn't handle non-finite values.
Results may differ from the reference program's by a relative error of at most 0.0003.
Values sent between devices are 32-bit elements; how exact they have to be, the bound alone decides.
A program may use at most 64 MiB of HBM per device.

```python
import math
import jax
import jax.numpy as jnp
from jax import lax

Q = 512
DRIVES = 2
NDIP = 32768


def draw_positions(key, part):
    ordinal = jnp.arange(NDIP, dtype=jnp.int32)
    column = (ordinal % 32).astype(jnp.float32)
    site_row = (ordinal // 32 % 32).astype(jnp.float32)
    depth_level = (ordinal // 1024).astype(jnp.float32)
    jitter_size = 0.2
    jitter = jax.random.uniform(key, (3, NDIP), jnp.float32, -jitter_size, jitter_size)
    return jnp.stack([column, site_row, depth_level]) + jitter


def shard_levels(rng, extent, split, least, largest):
    loudness, own = 1.0, jax.random.fold_in(rng, 6)
    for dim, shards_of in split:
        draws = jnp.exp(jax.random.uniform(jax.random.fold_in(own, dim), (shards_of,), jnp.float32, least / len(split), largest / len(split)))
        loudness = loudness * jnp.repeat(draws, extent[dim] // shards_of).reshape([-1 if axis == dim else 1 for axis in range(len(extent))])
    return loudness


def normal_values(rng, shape, deviation, reach, cuts=(), held_as=jnp.bfloat16):
    result = deviation * jax.random.normal(rng, shape, jnp.float32)
    if cuts:
        result = result * shard_levels(rng, shape, cuts, -0.22, 0.18)
    return jnp.clip(result, -reach, reach).astype(held_as)


def setup_inputs(seed: int = 0) -> dict:
    key_of = jax.random.split(jax.random.key(seed), 8)
    return {
        "positions": draw_positions(jax.random.fold_in(key_of[7], 71), 0),
        "moments": normal_values(key_of[1], (DRIVES, 2, 3, NDIP), 1.0, 6.0, ((3, 512),), jnp.float32),
        "inv_polar_re": jnp.clip(jnp.exp(math.log(2.0) - 1.3862944 * jax.random.uniform(key_of[2], (NDIP,), jnp.float32) ** shard_levels(key_of[2], (NDIP,), ((0, 512),), -0.2, 0.2)), 0.5, 2.0),
        "inv_polar_im": jnp.clip(jax.random.uniform(key_of[3], (NDIP,), jnp.float32, -0.5, 0.5) * shard_levels(key_of[3], (NDIP,), ((0, 512),), -0.4, 0.0), -0.5, 0.5),
        "mode_field": normal_values(key_of[4], (2, 3, NDIP, Q), (0.27 / (Q * 6 * NDIP) ** 0.25), 0.0390625, ((2, 512),), jnp.float32),
        "mode_detune": jnp.clip(jax.random.uniform(key_of[5], (Q,), jnp.float32, -1.0, 1.0), -1.0, 1.0),
        "mode_width": jnp.clip(jnp.exp(jax.random.uniform(key_of[6], (Q,), jnp.float32, math.log(0.05), math.log(1.0))), 0.05, 1.0),
    }


wavenumber = 1.0
coupling = 0.05
near_limit = 0.04

def pair_field(deltas, dipoles, axis_sum):
    delta_x, delta_y, delta_z = deltas
    square = delta_x * delta_x + delta_y * delta_y + delta_z * delta_z
    coincide = square < near_limit
    safe_square = jnp.where(coincide, 1.0, square)
    inverse = 1.0 / jnp.sqrt(safe_square)
    phase_arg = wavenumber * safe_square * inverse
    cos_val = jnp.cos(phase_arg)
    sine_val = jnp.sin(phase_arg)
    masked_cube = jnp.where(coincide, 0.0, inverse * inverse * inverse)
    near_re = phase_arg * phase_arg - 1.0
    far_re = 3.0 - phase_arg * phase_arg
    diag_re = (cos_val * near_re - sine_val * phase_arg) * masked_cube
    diag_im = (sine_val * near_re + cos_val * phase_arg) * masked_cube
    scaled = masked_cube / safe_square
    outer_re = (cos_val * far_re + 3.0 * sine_val * phase_arg) * scaled
    outer_im = (sine_val * far_re - 3.0 * cos_val * phase_arg) * scaled
    tile_list = []
    for drive_set in range(len(dipoles) // 6):
        moment_re = dipoles[6 * drive_set:6 * drive_set + 3]
        moment_im = dipoles[6 * drive_set + 3:6 * drive_set + 6]
        proj_re = delta_x * moment_re[0] + delta_y * moment_re[1] + delta_z * moment_re[2]
        proj_im = delta_x * moment_im[0] + delta_y * moment_im[1] + delta_z * moment_im[2]
        along_re = outer_re * proj_re - outer_im * proj_im
        along_im = outer_re * proj_im + outer_im * proj_re
        for component in range(3):
            tile_list.append(diag_re * moment_re[component] - diag_im * moment_im[component] + deltas[component] * along_re)
        for component in range(3):
            tile_list.append(diag_re * moment_im[component] + diag_im * moment_re[component] + deltas[component] * along_im)
    return jnp.stack([lax.optimization_barrier(jnp.sum(entry_tile, axis=axis_sum)) for entry_tile in tile_list])

def contract(left, right):
    return lax.dot_general(left, right, (((0,), (1,)), ((), ())), precision=lax.Precision.HIGHEST)

def modal_project(mode_rows, moment_rows):
    amp_re = contract(mode_rows[0], moment_rows[:, 0]) - contract(mode_rows[1], moment_rows[:, 1])
    amp_im = contract(mode_rows[0], moment_rows[:, 1]) + contract(mode_rows[1], moment_rows[:, 0])
    return (amp_re, amp_im)

def spread(weights, rows):
    return lax.dot_general(weights, rows, (((0,), (1,)), ((), ())), precision=lax.Precision.HIGHEST)

def modal_spread(mode_rows, amp_re, amp_im, mode_detune, mode_width):
    denominator = mode_detune * mode_detune + mode_width * mode_width
    resp_re = (mode_detune / denominator)[:, None]
    resp_im = (mode_width / denominator)[:, None]
    weighted_re = resp_re * amp_re - resp_im * amp_im
    weighted_im = resp_re * amp_im + resp_im * amp_re
    out_re = spread(weighted_re, mode_rows[0]) - spread(weighted_im, mode_rows[1])
    out_im = spread(weighted_re, mode_rows[1]) + spread(weighted_im, mode_rows[0])
    return jnp.stack([out_re, out_im], axis=1)

def combine(moments, inv_polar_re, inv_polar_im, pair_part, modal_part):
    drives = moments.shape[0]
    dipole_count = moments.shape[3]
    field_sum = coupling * pair_part.reshape(drives, 2, 3, dipole_count) + modal_part.reshape(drives, 2, 3, dipole_count)
    moment_re = moments[:, 0]
    moment_im = moments[:, 1]
    resp_re = inv_polar_re * moment_re - inv_polar_im * moment_im - field_sum[:, 0]
    resp_im = inv_polar_re * moment_im + inv_polar_im * moment_re - field_sum[:, 1]
    return jnp.stack([resp_re, resp_im], axis=1)

def reference(positions, moments, inv_polar_re, inv_polar_im, mode_field, mode_detune, mode_width):
    drives = moments.shape[0]
    dipole_count = positions.shape[1]
    flat_moments = moments.reshape(drives * 6, dipole_count)
    source_mom = [flat_moments[member][None, :] for member in range(drives * 6)]
    block_rows = math.gcd(dipole_count, 128)

    def one_block(offset):
        target_pos = lax.dynamic_slice_in_dim(positions, offset, block_rows, 1)
        deltas = [target_pos[axis_c][:, None] - positions[axis_c][None, :] for axis_c in range(3)]
        return pair_field(deltas, source_mom, 1)
    starts = jnp.arange(dipole_count // block_rows, dtype=jnp.int32) * block_rows
    blocks = lax.map(one_block, starts)
    pair_part = jnp.transpose(blocks, (1, 0, 2)).reshape(drives * 6, dipole_count)
    mode_rows = mode_field.reshape(2, 3 * dipole_count, mode_field.shape[3])
    amp_re, amp_im = modal_project(mode_rows, moments.reshape(drives, 2, 3 * dipole_count))
    modal_part = modal_spread(mode_rows, amp_re, amp_im, mode_detune, mode_width).reshape(drives * 6, dipole_count)
    return combine(moments, inv_polar_re, inv_polar_im, pair_part, modal_part)
```

```python
import math

import jax
import jax.numpy as jnp
import numpy as np
from jax import lax
from jax.experimental import pallas as pl
from jax.experimental.pallas import tpu as pltpu
from jax.sharding import PartitionSpec as P

F32, BF16 = jnp.float32, jnp.bfloat16
MESH = pl.DeviceIdType.MESH
KAPPA = 1.0 / (2.0 * math.pi)
COUPLING = 0.05
SHIFT = 1.25
HUGE = 1e30


def feature_maps():
    e = np.zeros((4, 160, 96), np.float32)
    for c in range(4):
        delta = (c - 1.5) * SHIFT
        base = np.zeros((160, 32), np.float32)
        for d in range(2):
            for j in range(15):
                row = j * 2 + d
                if j < 3:
                    base[row, 3] = 1.0; comp = j
                elif j < 12:
                    a, comp = divmod(j - 3, 3)
                else:
                    a, comp = j - 12, None
                if j >= 3:
                    base[row, a] = 1.0
                    if a == 0: base[row, 3] = -delta
                for ri in range(2):
                    m = 4 + d * 6 + ri * 3
                    if comp is not None:
                        base[32 + 32 * ri + row, m + comp] = -3.0
                    else:
                        base[32 + 32 * ri + row, 16 + d * 2 + ri] = -3.0
                        base[32 + 32 * ri + row, m] = 3.0 * delta
                        base[96 + 32 * ri + row, m + a] = 1.0
        for piece in range(3):
            e[c, :, 32 * piece:32 * piece + 32] = base
    return e


def pieces(v):
    h = v.astype(BF16).astype(F32)
    rest = v - h
    m = rest.astype(BF16).astype(F32)
    return h, m, rest - m


S4 = [4.442882834891087, -7.308241184594817, 3.6062893302761356, -0.8457653963567059, 0.10920874208169386]
C5 = [1.4142134965690698, -6.978850988398392, 5.73946117217025, -1.8835629909695983, 0.3106981907767927]

def planes(r2):
    y = lax.rsqrt(r2)
    w = r2 * y
    f = w - jnp.round(w)
    t = f * f
    s = S4[-1]
    for k in S4[-2::-1]: s = s * t + k
    s = s * f
    c = C5[-1]
    for k in C5[-2::-1]: c = c * t + k
    sy = s * y
    gr = y - s * sy
    gi = sy * c
    q = y * y
    u = y * KAPPA
    v1 = 1.0 - q * (KAPPA * KAPPA)
    ar = gr * v1 - gi * u
    ai = gi * v1 + gr * u
    br = q * (ar - (2.0 / 3.0) * gr)
    bi = q * (ai - (2.0 / 3.0) * gi)
    return ar, ai, br, bi


def split(v):
    h = v.astype(BF16)
    return h, (v - h.astype(F32)).astype(BF16)


def perm_map():
    m = np.zeros((64, 128), np.float32)
    for r in range(2):
        for c in range(4):
            for x in range(8):
                m[32 * r + 8 * c + x, 16 * c + 8 * r + x] = 1.0
    m[:, 64:] = m[:, :64]
    return m


def prep_targets(tpos, o_t, tag_dev, ta, xrow):
    lane8 = lax.broadcasted_iota(jnp.int32, (8, 128), 1)
    lane = lax.broadcasted_iota(jnp.int32, (8, 256), 1)
    sub = lax.broadcasted_iota(jnp.int32, (8, 256), 0)
    org = jnp.where(sub == 0, o_t[0], jnp.where(sub == 1, o_t[1], o_t[2]))
    jrow = lax.broadcasted_iota(jnp.int32, (64, 256), 0)
    jlane = lax.broadcasted_iota(jnp.int32, (64, 256), 1)
    for c in range(4):
        halves = []
        for t in range(2):
            v = jnp.zeros((8, 128), F32)
            for k in range(8):
                shift = (16 * (k - c)) % 128
                a = tpos[8 * t + k]
                if shift: a = pltpu.roll(a, shift, 1)
                v = jnp.where(lane8 // 16 == k, a, v)
            halves.append(v)
        raw = jnp.concatenate(halves, axis=1)
        delta = (c - 1.5) * SHIFT
        loc = (raw - org) * KAPPA - jnp.where(sub == 0, delta, 0.0)
        loc = jnp.where(sub < 3, loc, 0.0)
        xrow[c] = loc
        n2 = jnp.sum(loc * loc, axis=0, keepdims=True)
        v = jnp.where(sub == c, -2.0 * loc[0:1], jnp.where(sub == 4, -2.0 * loc[1:2], jnp.where(sub == 5, -2.0 * loc[2:3], jnp.where(sub == 6, n2, 0.0))))
        h, m, l = pieces(v)
        g6 = jnp.where((sub == c) | (sub == 4 + c), 1.0, 0.0)
        g7 = jnp.where(sub == c, 1.0, 0.0)
        tag = jnp.where((jlane // 16 == tag_dev) & (jrow == 16 * c + jlane % 16), HUGE, 0.0)
        ta[c] = jnp.concatenate([h, m, l, h, m, h, g6, g7, tag], axis=0).astype(BF16)


def prep_sources(src, slot, o_s, oy_r2, own_tag, emap, wmat, sb):
    low = lax.broadcasted_iota(jnp.int32, (8, 128), 1) < 64
    ra, rb = [], []
    for p in range(2):
        a, b = src[4 * slot + 2 * p], src[4 * slot + 2 * p + 1]
        ra.append(jnp.where(low, a, pltpu.roll(b, 64, 1)))
        rb.append(jnp.where(low, pltpu.roll(a, 64, 1), b))
    fa = jnp.concatenate(ra, axis=1)
    fb = jnp.concatenate(rb, axis=1)
    sub = lax.broadcasted_iota(jnp.int32, (8, 256), 0)
    org = jnp.where(sub == 0, o_s[0], jnp.where(sub == 1, o_s[1], o_s[2]))
    loc = (fa - org) * KAPPA
    yr2 = (fa[1:2] - oy_r2) * KAPPA
    f0 = jnp.where(sub < 3, loc, jnp.where(sub == 3, 1.0, fa))
    xs = [f0[k:k + 1] for k in range(3)]
    mom = [f0[4 + k:5 + k] for k in range(4)] + [fb[k:k + 1] for k in range(8)]
    us = []
    for d in range(2):
        for ri in range(2):
            b = d * 6 + ri * 3
            us.append(xs[0] * mom[b] + xs[1] * mom[b + 1] + xs[2] * mom[b + 2])
    f2 = jnp.concatenate(us + [jnp.zeros((4, 256), F32)], axis=0)
    feats = jnp.concatenate([f0, fb, f2, jnp.zeros((8, 256), F32)], axis=0)
    h, m, l = pieces(feats)
    frp = jnp.concatenate([h, m, l], axis=0).astype(BF16)
    for c in range(4):
        o = jnp.dot(emap[c], frp, preferred_element_type=F32)
        xe = o[:32]
        pr, pi = o[32:64] * xe, o[64:96] * xe
        ar, ai = o[96:128], o[128:160]
        for k, (re, im) in enumerate(((ar, ai), (pr, pi))):
            rh, rl = split(re); ih, il = split(im)
            wmat[c, :, pl.ds(512 * k, 256)] = jnp.concatenate([rh, ih, rl, il], axis=0)
            wmat[c, :, pl.ds(512 * k + 256, 256)] = jnp.concatenate([-ih, rh, -il, rl], axis=0)
    lane = lax.broadcasted_iota(jnp.int32, (64, 256), 1)
    j = lax.broadcasted_iota(jnp.int32, (64, 256), 0)
    tag = jnp.where(lane == own_tag + j, 1.0, 0.0)
    shift = (sub.astype(F32) - 1.5) * SHIFT
    va = jnp.where(sub < 4, xs[0] - shift, jnp.where(sub == 4, yr2, jnp.where(sub == 5, xs[2], jnp.where(sub == 6, 1.0, 0.0))))
    yz = yr2 * yr2 + xs[2] * xs[2]
    vb = jnp.where(sub < 4, va * va + yz, 0.0)
    ah, am, al = pieces(va); bh, bm, bl = pieces(vb)
    b6 = jnp.where(sub < 4, bh, pltpu.roll(bm, 4, 0))
    rows = jnp.concatenate([ah, ah, ah, am, am, al, b6, bl, tag], axis=0)
    sb[...] = jnp.concatenate([rows[:, :128].T, rows[:, 128:].T], axis=0).astype(BF16)


def finish(acc, xr, dy):
    t = acc[:64] + acc[64:]
    x = [xr[k:k + 1] for k in range(3)]
    x[1] = x[1] + dy
    out = [None] * 12
    for ri in range(2):
        row = lambda j: t[ri * 32 + 2 * j:ri * 32 + 2 * j + 2]
        s1 = [row(k) for k in range(3)]
        s2 = [[row(3 + 3 * a + k) for k in range(3)] for a in range(3)]
        s3 = [row(12 + k) for k in range(3)]
        inner = x[0] * s1[0] + x[1] * s1[1] + x[2] * s1[2] - (s2[0][0] + s2[1][1] + s2[2][2])
        for c in range(3):
            val = s3[c] + x[c] * inner - (x[0] * s2[c][0] + x[1] * s2[c][1] + x[2] * s2[c][2])
            for d in range(2):
                out[d * 6 + ri * 3 + c] = val[d:d + 1]
    return jnp.concatenate(out, axis=0)


def nn(a, b):
    return lax.dot_general(a, b, (((1,), (0,)), ((), ())), precision=lax.Precision.HIGHEST, preferred_element_type=F32)


def nt(a, b):
    return lax.dot_general(a, b, (((1,), (1,)), ((), ())), precision=lax.Precision.HIGHEST, preferred_element_type=F32)


def permuted(rows, table):
    h, m, l = pieces(rows)
    n = rows.shape[0]
    o = jnp.dot(jnp.concatenate([h, m, l], axis=0).astype(BF16), table, preferred_element_type=F32)
    return o[:n] + o[n : 2 * n] + o[2 * n :]


def kernel(pos, mom, ipr, ipi, mode, det, wid, emap, perm, unperm, out,
           src, tgt, ta, xrow, wmat, sb, g, r2b, acc, amp, rs, zb, cb, ag, obuf, rbuf,
           tgt_s, tgt_r, src_s, src_r, fwd_s, fwd_r, rs_s, rs_r, zb_s, zb_r, cb_s, cb_r, ag_s, ag_r, o_s, o_r):
    blk, grp = lax.axis_index("blk"), lax.axis_index("grp")
    zl, x, zh, y, core = blk // 4, blk % 4, grp // 8, (grp // 2) % 4, grp % 2
    me_r, me_z = x * 4 + y, zh * 8 + zl

    def at_r(r):
        return (zl * 4 + r // 4, zh * 8 + (r % 4) * 2 + core)

    def at_z(z):
        return ((z % 8) * 4 + x, (z // 8) * 8 + y * 2 + core)

    sibling = (blk, zh * 8 + y * 2 + (1 - core))

    barrier = pltpu.get_barrier_semaphore()

    def greet(s, _):
        pl.semaphore_signal(barrier, inc=1, device_id=at_r((me_r + s) % 16), device_id_type=MESH)
        pl.semaphore_signal(barrier, inc=1, device_id=at_z((me_z + s) % 16), device_id_type=MESH)
        return 0

    lax.fori_loop(1, 16, greet, 0)
    pl.semaphore_signal(barrier, inc=1, device_id=sibling, device_id_type=MESH)

    def remote(a, b, ss, rr, dev):
        return pltpu.make_async_remote_copy(src_ref=a, dst_ref=b, send_sem=ss, recv_sem=rr, device_id=dev, device_id_type=MESH)

    def spread_to(buf, ss, rr, me, where):
        def go(s, _):
            j = (me + s) % 16
            remote(buf.at[me], buf.at[me], ss.at[j], rr.at[me], where(j)).start()
            return 0
        lax.fori_loop(1, 16, go, 0)

    def arrived(buf, ss, rr, me, where):
        def go(s, _):
            j = (me + s) % 16
            remote(buf.at[j], buf.at[j], ss.at[j], rr.at[j], where(j)).wait_recv()
            return 0
        lax.fori_loop(1, 16, go, 0)

    def sent(buf, ss, rr, me, where):
        def go(s, _):
            j = (me + s) % 16
            remote(buf.at[me], buf.at[me], ss.at[j], rr.at[me], where(j)).wait_send()
            return 0
        lax.fori_loop(1, 16, go, 0)

    feats = jnp.concatenate([pos[...], jnp.ones((1, 64), F32)] + [mom[d, ri] for d in range(2) for ri in range(2)], axis=0)
    moved = permuted(feats, perm[...])
    low = lax.broadcasted_iota(jnp.int32, (8, 128), 1) < 64
    tile = jnp.where(low, moved[:8], moved[8:])
    src[core, me_z] = tile
    tgt[me_r] = tile

    pa, pb = 0.0, 0.0
    for c in range(3):
        pc = jnp.concatenate([mom[d, ri, c : c + 1] for d in range(2) for ri in range(2)], axis=0)
        pa = pa + nn(pc, mode[0, c])
        pb = pb + nn(pc, mode[1, c])
    for d in range(2):
        re = pa[2 * d : 2 * d + 1] - pb[2 * d + 1 : 2 * d + 2]
        im = pa[2 * d + 1 : 2 * d + 2] + pb[2 * d : 2 * d + 1]
        for q in range(4):
            amp[8 * d + q] = re[:, 128 * q : 128 * q + 128]
            amp[8 * d + 4 + q] = im[:, 128 * q : 128 * q + 128]

    pl.semaphore_wait(barrier, 31)

    mine = src.at[core]
    spread_to(tgt, tgt_s, tgt_r, me_r, at_r)
    spread_to(mine, src_s, src_r, me_z, at_z)

    def scatter(s, _):
        j = (me_r + s) % 16
        remote(amp.at[j], rs.at[me_r], rs_s.at[j], rs_r.at[me_r], at_r(j)).start()
        return 0

    lax.fori_loop(1, 16, scatter, 0)
    rs[me_r] = amp[me_r]

    ox, oz, oyt = 15.5, 4.0 * zl.astype(F32) + 1.5, (16 * zh + 2 * core).astype(F32) + 6.5
    arrived(tgt, tgt_s, tgt_r, me_r, at_r)
    prep_targets(tgt, (ox, oyt, oz), me_r, ta, xrow)
    acc[...] = jnp.zeros_like(acc)

    def one_block(step, _):
        quad = (me_z // 4 + step) % 4
        away = step // 4
        from_core = (core + away) % 2
        quad_ref = src.at[from_core, pl.ds(4 * quad, 4)]

        @pl.when(away == 0)
        def _():
            def go(k, _):
                z = 4 * quad + k
                @pl.when(z != me_z)
                def _():
                    remote(mine.at[z], mine.at[z], src_s.at[z], src_r.at[z], at_z(z)).wait_recv()
                return 0
            lax.fori_loop(0, 4, go, 0)
            remote(quad_ref, quad_ref, fwd_s.at[quad], fwd_r.at[quad], sibling).start()

        @pl.when(away == 1)
        def _():
            remote(quad_ref, quad_ref, fwd_s.at[quad], fwd_r.at[quad], sibling).wait_recv()

        half = quad // 2
        oys = (16 * half + 4 * y).astype(F32) + 1.5
        own = jnp.where(step == 0, (me_z % 4) * 64, -1000)
        prep_sources(src.at[from_core], quad, (ox, oys, oz), oyt, own, emap, wmat, sb)
        for c in range(4):
            r2b[...] = jnp.dot(sb[...], ta[c], preferred_element_type=F32)
            for k in range(16):
                for n, v in enumerate(planes(r2b[16 * k : 16 * k + 16, :])):
                    h, l = split(v)
                    g[0, 256 * n + 16 * k : 256 * n + 16 * k + 16, :] = h
                    g[1, 256 * n + 16 * k : 256 * n + 16 * k + 16, :] = l
            w = wmat[c]
            acc[half, c] += jnp.dot(w, g[0], preferred_element_type=F32) + jnp.dot(w, g[1], preferred_element_type=F32)

        @pl.when(step == 1)
        def _():
            arrived(rs, rs_s, rs_r, me_r, at_r)
            zb[me_z] = jnp.sum(rs[...], axis=0)
            spread_to(zb, zb_s, zb_r, me_z, at_z)

        @pl.when(step == 4)
        def _():
            arrived(zb, zb_s, zb_r, me_z, at_z)
            cb[core] = jnp.sum(zb[...], axis=0)
            remote(cb.at[core], cb.at[core], cb_s.at[0], cb_r.at[0], sibling).start()

        @pl.when(step == 5)
        def _():
            remote(cb.at[1 - core], cb.at[1 - core], cb_s.at[0], cb_r.at[0], sibling).wait_recv()
            ag[me_r] = cb[0] + cb[1]
            spread_to(ag, ag_s, ag_r, me_r, at_r)

        return 0

    lax.fori_loop(0, 8, one_block, 0)

    lane = lax.broadcasted_iota(jnp.int32, (8, 128), 1)
    fa, fb = [], []
    for c in range(4):
        f = 0.0
        for half in range(2):
            dy = (oyt - ((16 * half + 4 * y).astype(F32) + 1.5)) * KAPPA
            f = f + finish(acc[half, c], xrow[c], dy)
        fa.append(f[:8])
        fb.append(jnp.concatenate([f[8:], jnp.zeros((4, 256), F32)], axis=0))
    for r in range(16):
        t, k = r // 8, r % 8
        v = jnp.zeros((8, 128), F32)
        for c in range(4):
            for top, rows in ((0, fa[c]), (64, fb[c])):
                a = rows[:, 128 * t : 128 * t + 128]
                shift = (top + 16 * (c - k)) % 128
                if shift:
                    a = pltpu.roll(a, shift, 1)
                v = jnp.where(lane // 16 == top // 16 + c, a, v)
        obuf[r] = v

    def give(s, _):
        j = (me_r + s) % 16
        remote(obuf.at[j], rbuf.at[me_r], o_s.at[j], o_r.at[me_r], at_r(j)).start()
        return 0

    lax.fori_loop(1, 16, give, 0)
    rbuf[me_r] = obuf[me_r]

    arrived(ag, ag_s, ag_r, me_r, at_r)
    rows = [jnp.concatenate([ag[4 * k + q] for q in range(4)], axis=1) for k in range(4)]
    den = det[...] * det[...] + wid[...] * wid[...]
    rr, ri = det[...] / den, wid[...] / den
    weighted = []
    for d in range(2):
        re, im = rows[2 * d], rows[2 * d + 1]
        weighted += [rr * re - ri * im, rr * im + ri * re]
    weighted = jnp.concatenate(weighted, axis=0)
    part = []
    for c in range(3):
        part.append((nt(weighted, mode[0, c]), nt(weighted, mode[1, c])))

    sent(tgt, tgt_s, tgt_r, me_r, at_r)
    sent(mine, src_s, src_r, me_z, at_z)
    sent(zb, zb_s, zb_r, me_z, at_z)
    sent(ag, ag_s, ag_r, me_r, at_r)

    def settle(s, _):
        j = (me_r + s) % 16
        remote(amp.at[j], rs.at[me_r], rs_s.at[j], rs_r.at[me_r], at_r(j)).wait_send()
        remote(obuf.at[j], rbuf.at[me_r], o_s.at[j], o_r.at[me_r], at_r(j)).wait_send()
        return 0

    lax.fori_loop(1, 16, settle, 0)
    remote(cb.at[core], cb.at[core], cb_s.at[0], cb_r.at[0], sibling).wait_send()

    def settle_quads(q, _):
        quad_ref = mine.at[pl.ds(4 * q, 4)]
        remote(quad_ref, quad_ref, fwd_s.at[q], fwd_r.at[q], sibling).wait_send()
        return 0

    lax.fori_loop(0, 4, settle_quads, 0)
    arrived(rbuf, o_s, o_r, me_r, at_r)
    total = jnp.sum(rbuf[...], axis=0)
    total = jnp.concatenate([total, pltpu.roll(total, 64, 1)], axis=0)[:, :64]
    field = permuted(total, unperm[...]) * (COUPLING * KAPPA)
    pr, pi = ipr[...], ipi[...]
    for d in range(2):
        for c in range(3):
            a, b = part[c]
            pre, pim = mom[d, 0, c : c + 1], mom[d, 1, c : c + 1]
            k = 6 * d + c
            mre = a[2 * d : 2 * d + 1] - b[2 * d + 1 : 2 * d + 2]
            mim = a[2 * d + 1 : 2 * d + 2] + b[2 * d : 2 * d + 1]
            out[d, 0, c : c + 1] = pr * pre - pi * pim - field[k : k + 1, :64] - mre
            out[d, 1, c : c + 1] = pr * pim + pi * pre - field[k + 3 : k + 4, :64] - mim


def on_device(positions, moments, inv_polar_re, inv_polar_im, mode_field, mode_detune, mode_width):
    table = perm_map()
    back = np.zeros((64, 128), np.float32)
    back[:, :64] = table[:, :64].T
    vm = pl.BlockSpec(memory_space=pltpu.VMEM)
    dma = lambda n: pltpu.SemaphoreType.DMA((n,))
    return pl.pallas_call(
        kernel,
        out_shape=jax.ShapeDtypeStruct(moments.shape, F32),
        in_specs=[vm] * 10,
        out_specs=vm,
        scratch_shapes=[
            pltpu.VMEM((2, 16, 8, 128), F32),
            pltpu.VMEM((16, 8, 128), F32),
            pltpu.VMEM((4, 128, 256), BF16),
            pltpu.VMEM((4, 8, 256), F32),
            pltpu.VMEM((4, 128, 1024), BF16),
            pltpu.VMEM((256, 128), BF16),
            pltpu.VMEM((2, 1024, 256), BF16),
            pltpu.VMEM((256, 256), F32),
            pltpu.VMEM((2, 4, 128, 256), F32),
            pltpu.VMEM((16, 1, 128), F32),
            pltpu.VMEM((16, 1, 128), F32),
            pltpu.VMEM((16, 1, 128), F32),
            pltpu.VMEM((2, 1, 128), F32),
            pltpu.VMEM((16, 1, 128), F32),
            pltpu.VMEM((16, 8, 128), F32),
            pltpu.VMEM((16, 8, 128), F32),
        ]
        + [dma(16), dma(16), dma(16), dma(16), dma(4), dma(4), dma(16), dma(16)]
        + [dma(16), dma(16), dma(1), dma(1), dma(16), dma(16), dma(16), dma(16)],
        compiler_params=pltpu.CompilerParams(collective_id=0, has_side_effects=True, vmem_limit_bytes=48 << 20),
    )(
        positions,
        moments,
        inv_polar_re.reshape(1, -1),
        inv_polar_im.reshape(1, -1),
        mode_field,
        mode_detune.reshape(1, -1),
        mode_width.reshape(1, -1),
        jnp.asarray(feature_maps(), BF16),
        jnp.asarray(table, BF16),
        jnp.asarray(back, BF16),
    )


def solution(mesh):
    both = ("blk", "grp")
    placed = (P(None, both), P(None, None, None, both), P(both), P(both), P(None, None, both, None), P(), P())
    return jax.shard_map(on_device, mesh=mesh, in_specs=placed, out_specs=P(None, None, None, both), check_vma=False)
```

```python
import math

import jax
import jax.numpy as jnp
import numpy as np
from jax import lax
from jax.experimental import pallas as pl
from jax.experimental.pallas import tpu as pltpu
from jax.sharding import PartitionSpec as P

F32, BF16 = jnp.float32, jnp.bfloat16
MESH = pl.DeviceIdType.MESH
KAPPA = 1.0 / (2.0 * math.pi)
COUPLING = 0.05
SHIFT = 1.25
HUGE = 1e30


def feature_maps():
    e = np.zeros((4, 160, 96), np.float32)
    for c in range(4):
        delta = (c - 1.5) * SHIFT
        base = np.zeros((160, 32), np.float32)
        for d in range(2):
            for j in range(15):
                row = j * 2 + d
                if j < 3:
                    base[row, 3] = 1.0; comp = j
                elif j < 12:
                    a, comp = divmod(j - 3, 3)
                else:
                    a, comp = j - 12, None
                if j >= 3:
                    base[row, a] = 1.0
                    if a == 0: base[row, 3] = -delta
                for ri in range(2):
                    m = 4 + d * 6 + ri * 3
                    if comp is not None:
                        base[32 + 32 * ri + row, m + comp] = -3.0
                    else:
                        base[32 + 32 * ri + row, 16 + d * 2 + ri] = -3.0
                        base[32 + 32 * ri + row, m] = 3.0 * delta
                        base[96 + 32 * ri + row, m + a] = 1.0
        for piece in range(3):
            e[c, :, 32 * piece:32 * piece + 32] = base
    return e


def pieces(v):
    h = v.astype(BF16).astype(F32)
    rest = v - h
    m = rest.astype(BF16).astype(F32)
    return h, m, rest - m


S4 = [4.442882834891087, -7.308241184594817, 3.6062893302761356, -0.8457653963567059, 0.10920874208169386]
C5 = [1.4142134965690698, -6.978850988398392, 5.73946117217025, -1.8835629909695983, 0.3106981907767927]

def planes(r2):
    y = lax.rsqrt(r2)
    w = r2 * y
    f = w - jnp.round(w)
    t = f * f
    s = S4[-1]
    for k in S4[-2::-1]: s = s * t + k
    s = s * f
    c = C5[-1]
    for k in C5[-2::-1]: c = c * t + k
    sy = s * y
    gr = y - s * sy
    gi = sy * c
    q = y * y
    u = y * KAPPA
    v1 = 1.0 - q * (KAPPA * KAPPA)
    ar = gr * v1 - gi * u
    ai = gi * v1 + gr * u
    br = q * (ar - (2.0 / 3.0) * gr)
    bi = q * (ai - (2.0 / 3.0) * gi)
    return ar, ai, br, bi


def split(v):
    h = v.astype(BF16)
    return h, (v - h.astype(F32)).astype(BF16)


def perm_map():
    m = np.zeros((64, 128), np.float32)
    for r in range(2):
        for c in range(4):
            for x in range(8):
                m[32 * r + 8 * c + x, 16 * c + 8 * r + x] = 1.0
    m[:, 64:] = m[:, :64]
    return m


def prep_targets(tpos, o_t, tag_dev, ta, xrow):
    lane8 = lax.broadcasted_iota(jnp.int32, (8, 128), 1)
    lane = lax.broadcasted_iota(jnp.int32, (8, 256), 1)
    sub = lax.broadcasted_iota(jnp.int32, (8, 256), 0)
    org = jnp.where(sub == 0, o_t[0], jnp.where(sub == 1, o_t[1], o_t[2]))
    jrow = lax.broadcasted_iota(jnp.int32, (64, 256), 0)
    jlane = lax.broadcasted_iota(jnp.int32, (64, 256), 1)
    for c in range(4):
        halves = []
        for t in range(2):
            v = jnp.zeros((8, 128), F32)
            for k in range(8):
                shift = (16 * (k - c)) % 128
                a = tpos[8 * t + k]
                if shift: a = pltpu.roll(a, shift, 1)
                v = jnp.where(lane8 // 16 == k, a, v)
            halves.append(v)
        raw = jnp.concatenate(halves, axis=1)
        delta = (c - 1.5) * SHIFT
        loc = (raw - org) * KAPPA - jnp.where(sub == 0, delta, 0.0)
        loc = jnp.where(sub < 3, loc, 0.0)
        xrow[c] = loc
        n2 = jnp.sum(loc * loc, axis=0, keepdims=True)
        v = jnp.where(sub == c, -2.0 * loc[0:1], jnp.where(sub == 4, -2.0 * loc[1:2], jnp.where(sub == 5, -2.0 * loc[2:3], jnp.where(sub == 6, n2, 0.0))))
        h, m, l = pieces(v)
        g6 = jnp.where((sub == c) | (sub == 4 + c), 1.0, 0.0)
        g7 = jnp.where(sub == c, 1.0, 0.0)
        tag = jnp.where((jlane // 16 == tag_dev) & (jrow == 16 * c + jlane % 16), HUGE, 0.0)
        ta[c] = jnp.concatenate([h, m, l, h, m, h, g6, g7, tag], axis=0).astype(BF16)


def prep_sources(src, slot, o_s, oy_r2, own_tag, emap, wmat, sb):
    low = lax.broadcasted_iota(jnp.int32, (8, 128), 1) < 64
    ra, rb = [], []
    for p in range(2):
        a, b = src[4 * slot + 2 * p], src[4 * slot + 2 * p + 1]
        ra.append(jnp.where(low, a, pltpu.roll(b, 64, 1)))
        rb.append(jnp.where(low, pltpu.roll(a, 64, 1), b))
    fa = jnp.concatenate(ra, axis=1)
    fb = jnp.concatenate(rb, axis=1)
    sub = lax.broadcasted_iota(jnp.int32, (8, 256), 0)
    org = jnp.where(sub == 0, o_s[0], jnp.where(sub == 1, o_s[1], o_s[2]))
    loc = (fa - org) * KAPPA
    yr2 = (fa[1:2] - oy_r2) * KAPPA
    f0 = jnp.where(sub < 3, loc, jnp.where(sub == 3, 1.0, fa))
    xs = [f0[k:k + 1] for k in range(3)]
    mom = [f0[4 + k:5 + k] for k in range(4)] + [fb[k:k + 1] for k in range(8)]
    us = []
    for d in range(2):
        for ri in range(2):
            b = d * 6 + ri * 3
            us.append(xs[0] * mom[b] + xs[1] * mom[b + 1] + xs[2] * mom[b + 2])
    f2 = jnp.concatenate(us + [jnp.zeros((4, 256), F32)], axis=0)
    feats = jnp.concatenate([f0, fb, f2, jnp.zeros((8, 256), F32)], axis=0)
    h, m, l = pieces(feats)
    frp = jnp.concatenate([h, m, l], axis=0).astype(BF16)
    for c in range(4):
        o = jnp.dot(emap[c], frp, preferred_element_type=F32)
        xe = o[:32]
        pr, pi = o[32:64] * xe, o[64:96] * xe
        ar, ai = o[96:128], o[128:160]
        for k, (re, im) in enumerate(((ar, ai), (pr, pi))):
            rh, rl = split(re); ih, il = split(im)
            wmat[c, :, pl.ds(512 * k, 256)] = jnp.concatenate([rh, ih, rl, il], axis=0)
            wmat[c, :, pl.ds(512 * k + 256, 256)] = jnp.concatenate([-ih, rh, -il, rl], axis=0)
    lane = lax.broadcasted_iota(jnp.int32, (64, 256), 1)
    j = lax.broadcasted_iota(jnp.int32, (64, 256), 0)
    tag = jnp.where(lane == own_tag + j, 1.0, 0.0)
    shift = (sub.astype(F32) - 1.5) * SHIFT
    va = jnp.where(sub < 4, xs[0] - shift, jnp.where(sub == 4, yr2, jnp.where(sub == 5, xs[2], jnp.where(sub == 6, 1.0, 0.0))))
    yz = yr2 * yr2 + xs[2] * xs[2]
    vb = jnp.where(sub < 4, va * va + yz, 0.0)
    ah, am, al = pieces(va); bh, bm, bl = pieces(vb)
    b6 = jnp.where(sub < 4, bh, pltpu.roll(bm, 4, 0))
    rows = jnp.concatenate([ah, ah, ah, am, am, al, b6, bl, tag], axis=0)
    sb[...] = jnp.concatenate([rows[:, :128].T, rows[:, 128:].T], axis=0).astype(BF16)


def finish(acc, xr, dy):
    t = acc[:64] + acc[64:]
    x = [xr[k:k + 1] for k in range(3)]
    x[1] = x[1] + dy
    out = [None] * 12
    for ri in range(2):
        row = lambda j: t[ri * 32 + 2 * j:ri * 32 + 2 * j + 2]
        s1 = [row(k) for k in range(3)]
        s2 = [[row(3 + 3 * a + k) for k in range(3)] for a in range(3)]
        s3 = [row(12 + k) for k in range(3)]
        inner = x[0] * s1[0] + x[1] * s1[1] + x[2] * s1[2] - (s2[0][0] + s2[1][1] + s2[2][2])
        for c in range(3):
            val = s3[c] + x[c] * inner - (x[0] * s2[c][0] + x[1] * s2[c][1] + x[2] * s2[c][2])
            for d in range(2):
                out[d * 6 + ri * 3 + c] = val[d:d + 1]
    return jnp.concatenate(out, axis=0)


def nn(a, b):
    return lax.dot_general(a, b, (((1,), (0,)), ((), ())), precision=lax.Precision.HIGHEST, preferred_element_type=F32)


def nt(a, b):
    return lax.dot_general(a, b, (((1,), (1,)), ((), ())), precision=lax.Precision.HIGHEST, preferred_element_type=F32)


def permuted(rows, table):
    h, m, l = pieces(rows)
    n = rows.shape[0]
    o = jnp.dot(jnp.concatenate([h, m, l], axis=0).astype(BF16), table, preferred_element_type=F32)
    return o[:n] + o[n : 2 * n] + o[2 * n :]


def kernel(pos_h, mom_h, ipr_h, ipi_h, mode_h, det_h, wid_h, emap_h, perm_h, unperm_h, out,
           pos, mom, ipr, ipi, mode, det, wid, emap, perm, unperm, in_sem,
           src, tgt, ta, xrow, wmat, sb, ga, gb, ra, rb, acc, amp, rs, zb, cb, ag, obuf, rbuf,
           tgt_s, tgt_r, src_s, src_r, fwd_s, fwd_r, rs_s, rs_r, zb_s, zb_r, cb_s, cb_r, ag_s, ag_r, o_s, o_r):
    blk, grp = lax.axis_index("blk"), lax.axis_index("grp")
    zl, x, zh, y, core = blk // 4, blk % 4, grp // 8, (grp // 2) % 4, grp % 2
    me_r, me_z = x * 4 + y, zh * 8 + zl

    def at_r(r):
        return (zl * 4 + r // 4, zh * 8 + (r % 4) * 2 + core)

    def at_z(z):
        return ((z % 8) * 4 + x, (z // 8) * 8 + y * 2 + core)

    sibling = (blk, zh * 8 + y * 2 + (1 - core))

    barrier = pltpu.get_barrier_semaphore()

    def greet(s, _):
        pl.semaphore_signal(barrier, inc=1, device_id=at_r((me_r + s) % 16), device_id_type=MESH)
        pl.semaphore_signal(barrier, inc=1, device_id=at_z((me_z + s) % 16), device_id_type=MESH)
        return 0

    lax.fori_loop(1, 16, greet, 0, unroll=5)
    pl.semaphore_signal(barrier, inc=1, device_id=sibling, device_id_type=MESH)

    fetched = [
        pltpu.make_async_copy(a, b, in_sem.at[k])
        for k, (a, b) in enumerate(
            zip(
                (pos_h, mom_h, perm_h, mode_h, emap_h, det_h, wid_h, ipr_h, ipi_h, unperm_h),
                (pos, mom, perm, mode, emap, det, wid, ipr, ipi, unperm),
            )
        )
    ]
    for copy in fetched:
        copy.start()

    def remote(a, b, ss, rr, dev):
        return pltpu.make_async_remote_copy(src_ref=a, dst_ref=b, send_sem=ss, recv_sem=rr, device_id=dev, device_id_type=MESH)

    def spread_to(buf, ss, rr, me, where):
        def go(s, _):
            j = (me + s) % 16
            remote(buf.at[me], buf.at[me], ss.at[j], rr.at[me], where(j)).start()
            return 0
        lax.fori_loop(1, 16, go, 0, unroll=5)

    def arrived(buf, ss, rr, me, where):
        def go(s, _):
            j = (me + s) % 16
            remote(buf.at[j], buf.at[j], ss.at[j], rr.at[j], where(j)).wait_recv()
            return 0
        lax.fori_loop(1, 16, go, 0)

    def sent(buf, ss, rr, me, where):
        def go(s, _):
            j = (me + s) % 16
            remote(buf.at[me], buf.at[me], ss.at[j], rr.at[me], where(j)).wait_send()
            return 0
        lax.fori_loop(1, 16, go, 0)

    for copy in fetched[:3]:
        copy.wait()
    feats = jnp.concatenate(
        [pos[...], jnp.ones((1, 64), F32)]
        + [mom[d, c, ri : ri + 1] for d in range(2) for ri in range(2) for c in range(3)],
        axis=0,
    )
    moved = permuted(feats, perm[...])
    low = lax.broadcasted_iota(jnp.int32, (8, 128), 1) < 64
    tile = jnp.where(low, moved[:8], moved[8:])
    src[core, me_z] = tile
    tgt[me_r] = tile

    fetched[3].wait()
    pa, pb = 0.0, 0.0
    for c in range(3):
        pc = jnp.concatenate([mom[d, c] for d in range(2)], axis=0)
        pa = pa + nn(pc, mode[0, c])
        pb = pb + nn(pc, mode[1, c])
    for d in range(2):
        re = pa[2 * d : 2 * d + 1] - pb[2 * d + 1 : 2 * d + 2]
        im = pa[2 * d + 1 : 2 * d + 2] + pb[2 * d : 2 * d + 1]
        for q in range(4):
            amp[8 * d + q] = re[:, 128 * q : 128 * q + 128]
            amp[8 * d + 4 + q] = im[:, 128 * q : 128 * q + 128]

    for copy in fetched[4:]:
        copy.wait()
    pl.semaphore_wait(barrier, 31)

    mine = src.at[core]
    spread_to(tgt, tgt_s, tgt_r, me_r, at_r)
    spread_to(mine, src_s, src_r, me_z, at_z)

    def scatter(s, _):
        j = (me_r + s) % 16
        remote(amp.at[j], rs.at[me_r], rs_s.at[j], rs_r.at[me_r], at_r(j)).start()
        return 0

    lax.fori_loop(1, 16, scatter, 0, unroll=5)
    rs[me_r] = amp[me_r]

    ox, oz, oyt = 15.5, 4.0 * zl.astype(F32) + 1.5, (16 * zh + 2 * core).astype(F32) + 6.5
    arrived(tgt, tgt_s, tgt_r, me_r, at_r)
    prep_targets(tgt, (ox, oyt, oz), me_r, ta, xrow)
    acc[...] = jnp.zeros_like(acc)
    gb[...] = jnp.zeros_like(gb)
    wmat[1, 3] = jnp.zeros((128, 1024), BF16)

    def stage(w, gold, gnew, rnow, nxt, rnext):
        total = None
        for q in range(8):
            ko = 256 * (q % 4)
            part = jnp.dot(w[:, ko : ko + 256], gold[q // 4, ko : ko + 256], preferred_element_type=F32)
            if nxt is not None and q % 4 == 0:
                top = 32 * q
                r2 = jnp.dot(sb[top : top + 128], ta[nxt], preferred_element_type=F32)
            for k in (2 * q, 2 * q + 1):
                for n, v in enumerate(planes(rnow[16 * k : 16 * k + 16, :])):
                    h, l = split(v)
                    gnew[0, 256 * n + 16 * k : 256 * n + 16 * k + 16, :] = h
                    gnew[1, 256 * n + 16 * k : 256 * n + 16 * k + 16, :] = l
            if nxt is not None and q % 4 == 0:
                rnext[top : top + 128] = r2
            total = part if total is None else total + part
        return total

    def one_block(step, _):
        quad = (me_z // 4 + step) % 4
        away = step // 4
        from_core = (core + away) % 2
        quad_ref = src.at[from_core, pl.ds(4 * quad, 4)]

        @pl.when(away == 0)
        def _():
            def go(k, _):
                z = 4 * quad + k
                @pl.when(z != me_z)
                def _():
                    remote(mine.at[z], mine.at[z], src_s.at[z], src_r.at[z], at_z(z)).wait_recv()
                return 0
            lax.fori_loop(0, 4, go, 0)
            remote(quad_ref, quad_ref, fwd_s.at[quad], fwd_r.at[quad], sibling).start()

        @pl.when(away == 1)
        def _():
            remote(quad_ref, quad_ref, fwd_s.at[quad], fwd_r.at[quad], sibling).wait_recv()

        half = quad // 2
        oys = (16 * half + 4 * y).astype(F32) + 1.5
        own = jnp.where(step == 0, (me_z % 4) * 64, -1000)
        par = step % 2
        prep_sources(src.at[from_core], quad, (ox, oys, oz), oyt, own, emap, wmat.at[par], sb)
        ra[...] = jnp.dot(sb[...], ta[0], preferred_element_type=F32)
        before = ((me_z // 4 + step + 3) % 4) // 2
        acc[before, 3] += stage(wmat.at[1 - par, 3], gb, ga, ra, 1, rb)
        acc[half, 0] += stage(wmat.at[par, 0], ga, gb, rb, 2, ra)
        acc[half, 1] += stage(wmat.at[par, 1], gb, ga, ra, 3, rb)
        acc[half, 2] += stage(wmat.at[par, 2], ga, gb, rb, None, None)

        @pl.when(step == 1)
        def _():
            arrived(rs, rs_s, rs_r, me_r, at_r)
            zb[me_z] = jnp.sum(rs[...], axis=0)
            spread_to(zb, zb_s, zb_r, me_z, at_z)

        @pl.when(step == 4)
        def _():
            arrived(zb, zb_s, zb_r, me_z, at_z)
            cb[core] = jnp.sum(zb[...], axis=0)
            remote(cb.at[core], cb.at[core], cb_s.at[0], cb_r.at[0], sibling).start()

        @pl.when(step == 5)
        def _():
            remote(cb.at[1 - core], cb.at[1 - core], cb_s.at[0], cb_r.at[0], sibling).wait_recv()
            ag[me_r] = cb[0] + cb[1]
            spread_to(ag, ag_s, ag_r, me_r, at_r)

        return 0

    lax.fori_loop(0, 8, one_block, 0)
    last = ((me_z // 4 + 3) % 4) // 2
    w = wmat[1, 3]
    acc[last, 3] += jnp.dot(w, gb[0], preferred_element_type=F32) + jnp.dot(w, gb[1], preferred_element_type=F32)

    lane = lax.broadcasted_iota(jnp.int32, (8, 128), 1)
    fa, fb = [], []
    for c in range(4):
        f = 0.0
        for half in range(2):
            dy = (oyt - ((16 * half + 4 * y).astype(F32) + 1.5)) * KAPPA
            f = f + finish(acc[half, c], xrow[c], dy)
        fa.append(f[:8])
        fb.append(jnp.concatenate([f[8:], jnp.zeros((4, 256), F32)], axis=0))
    for r in range(16):
        t, k = r // 8, r % 8
        v = jnp.zeros((8, 128), F32)
        for c in range(4):
            for top, rows in ((0, fa[c]), (64, fb[c])):
                a = rows[:, 128 * t : 128 * t + 128]
                shift = (top + 16 * (c - k)) % 128
                if shift:
                    a = pltpu.roll(a, shift, 1)
                v = jnp.where(lane // 16 == top // 16 + c, a, v)
        obuf[r] = v

    def give(s, _):
        j = (me_r + s) % 16
        remote(obuf.at[j], rbuf.at[me_r], o_s.at[j], o_r.at[me_r], at_r(j)).start()
        return 0

    lax.fori_loop(1, 16, give, 0, unroll=5)
    rbuf[me_r] = obuf[me_r]

    arrived(ag, ag_s, ag_r, me_r, at_r)
    rows = [jnp.concatenate([ag[4 * k + q] for q in range(4)], axis=1) for k in range(4)]
    den = det[...] * det[...] + wid[...] * wid[...]
    rr, ri = det[...] / den, wid[...] / den
    weighted = []
    for d in range(2):
        re, im = rows[2 * d], rows[2 * d + 1]
        weighted += [rr * re - ri * im, rr * im + ri * re]
    weighted = jnp.concatenate(weighted, axis=0)
    part = []
    for c in range(3):
        part.append((nt(weighted, mode[0, c]), nt(weighted, mode[1, c])))

    sent(tgt, tgt_s, tgt_r, me_r, at_r)
    sent(mine, src_s, src_r, me_z, at_z)
    sent(zb, zb_s, zb_r, me_z, at_z)
    sent(ag, ag_s, ag_r, me_r, at_r)

    def settle(s, _):
        j = (me_r + s) % 16
        remote(amp.at[j], rs.at[me_r], rs_s.at[j], rs_r.at[me_r], at_r(j)).wait_send()
        remote(obuf.at[j], rbuf.at[me_r], o_s.at[j], o_r.at[me_r], at_r(j)).wait_send()
        return 0

    lax.fori_loop(1, 16, settle, 0)
    remote(cb.at[core], cb.at[core], cb_s.at[0], cb_r.at[0], sibling).wait_send()

    def settle_quads(q, _):
        quad_ref = mine.at[pl.ds(4 * q, 4)]
        remote(quad_ref, quad_ref, fwd_s.at[q], fwd_r.at[q], sibling).wait_send()
        return 0

    lax.fori_loop(0, 4, settle_quads, 0)
    arrived(rbuf, o_s, o_r, me_r, at_r)
    total = jnp.sum(rbuf[...], axis=0)
    total = jnp.concatenate([total, pltpu.roll(total, 64, 1)], axis=0)[:, :64]
    field = permuted(total, unperm[...]) * (COUPLING * KAPPA)
    pr, pi = ipr[...], ipi[...]
    for d in range(2):
        for c in range(3):
            a, b = part[c]
            pre, pim = mom[d, c, 0:1], mom[d, c, 1:2]
            k = 6 * d + c
            mre = a[2 * d : 2 * d + 1] - b[2 * d + 1 : 2 * d + 2]
            mim = a[2 * d + 1 : 2 * d + 2] + b[2 * d : 2 * d + 1]
            out[d, c, 0:1] = pr * pre - pi * pim - field[k : k + 1, :64] - mre
            out[d, c, 1:2] = pr * pim + pi * pre - field[k + 3 : k + 4, :64] - mim


def on_device(positions, moments, inv_polar_re, inv_polar_im, mode_field, mode_detune, mode_width):
    table = perm_map()
    back = np.zeros((64, 128), np.float32)
    back[:, :64] = table[:, :64].T
    vm = pl.BlockSpec(memory_space=pltpu.VMEM)
    dma = lambda n: pltpu.SemaphoreType.DMA((n,))
    arrays = (
        positions,
        moments.transpose(0, 2, 1, 3),
        inv_polar_re.reshape(1, -1),
        inv_polar_im.reshape(1, -1),
        mode_field,
        mode_detune.reshape(1, -1),
        mode_width.reshape(1, -1),
        jnp.asarray(feature_maps(), BF16),
        jnp.asarray(table, BF16),
        jnp.asarray(back, BF16),
    )
    response = pl.pallas_call(
        kernel,
        out_shape=jax.ShapeDtypeStruct(arrays[1].shape, F32),
        in_specs=[pl.BlockSpec(memory_space=pl.ANY)] * 10,
        out_specs=vm,
        scratch_shapes=[pltpu.VMEM(a.shape, a.dtype) for a in arrays]
        + [
            dma(10),
            pltpu.VMEM((2, 16, 8, 128), F32),
            pltpu.VMEM((16, 8, 128), F32),
            pltpu.VMEM((4, 128, 256), BF16),
            pltpu.VMEM((4, 8, 256), F32),
            pltpu.VMEM((2, 4, 128, 1024), BF16),
            pltpu.VMEM((256, 128), BF16),
            pltpu.VMEM((2, 1024, 256), BF16),
            pltpu.VMEM((2, 1024, 256), BF16),
            pltpu.VMEM((256, 256), F32),
            pltpu.VMEM((256, 256), F32),
            pltpu.VMEM((2, 4, 128, 256), F32),
            pltpu.VMEM((16, 1, 128), F32),
            pltpu.VMEM((16, 1, 128), F32),
            pltpu.VMEM((16, 1, 128), F32),
            pltpu.VMEM((2, 1, 128), F32),
            pltpu.VMEM((16, 1, 128), F32),
            pltpu.VMEM((16, 8, 128), F32),
            pltpu.VMEM((16, 8, 128), F32),
        ]
        + [dma(16), dma(16), dma(16), dma(16), dma(4), dma(4), dma(16), dma(16)]
        + [dma(16), dma(16), dma(1), dma(1), dma(16), dma(16), dma(16), dma(16)],
        compiler_params=pltpu.CompilerParams(collective_id=0, has_side_effects=True, vmem_limit_bytes=60 << 20),
    )(*arrays)
    return response.transpose(0, 2, 1, 3)


def solution(mesh):
    both = ("blk", "grp")
    placed = (P(None, both), P(None, None, None, both), P(both), P(both), P(None, None, both, None), P(), P())
    return jax.shard_map(on_device, mesh=mesh, in_specs=placed, out_specs=P(None, None, None, both), check_vma=False)
```

```python
import math

import jax
import jax.numpy as jnp
import numpy as np
from jax import lax
from jax.experimental import pallas as pl
from jax.experimental.pallas import tpu as pltpu
from jax.sharding import PartitionSpec as P

F32, BF16 = jnp.float32, jnp.bfloat16
MESH = pl.DeviceIdType.MESH
KAPPA = 1.0 / (2.0 * math.pi)
COUPLING = 0.05
SHIFT = 1.25
HUGE = 1e30


def feature_maps():
    e = np.zeros((4, 160, 96), np.float32)
    for c in range(4):
        delta = (c - 1.5) * SHIFT
        base = np.zeros((160, 32), np.float32)
        for d in range(2):
            for j in range(15):
                row = j * 2 + d
                if j < 3:
                    base[row, 3] = 1.0; comp = j
                elif j < 12:
                    a, comp = divmod(j - 3, 3)
                else:
                    a, comp = j - 12, None
                if j >= 3:
                    base[row, a] = 1.0
                    if a == 0: base[row, 3] = -delta
                for ri in range(2):
                    m = 4 + d * 6 + ri * 3
                    if comp is not None:
                        base[32 + 32 * ri + row, m + comp] = -3.0
                    else:
                        base[32 + 32 * ri + row, 16 + d * 2 + ri] = -3.0
                        base[32 + 32 * ri + row, m] = 3.0 * delta
                        base[96 + 32 * ri + row, m + a] = 1.0
        for piece in range(3):
            e[c, :, 32 * piece:32 * piece + 32] = base
    return e


def pieces(v):
    h = v.astype(BF16).astype(F32)
    rest = v - h
    m = rest.astype(BF16).astype(F32)
    return h, m, rest - m


S4 = [4.442867982147176, -7.307445408741119, 3.59480206222511, -0.7844035161415288]
C5 = [1.4142134965690698, -6.978850988398392, 5.73946117217025, -1.8835629909695983, 0.3106981907767927]

def planes(r2):
    y = lax.rsqrt(r2)
    w = r2 * y
    f = w - jnp.round(w)
    t = f * f
    s = S4[-1]
    for k in S4[-2::-1]: s = s * t + k
    s = s * f
    c = C5[-1]
    for k in C5[-2::-1]: c = c * t + k
    y23 = y * (2.0 / 3.0)
    sy = s * y23
    gr = y23 - s * sy
    gi = sy * c
    q = y * y
    u = y * (1.5 * KAPPA)
    v1 = 1.5 - q * (1.5 * KAPPA * KAPPA)
    ar = gr * v1 - gi * u
    ai = gi * v1 + gr * u
    br = q * (ar - gr)
    bi = q * (ai - gi)
    return ar, ai, br, bi


def split(v):
    h = v.astype(BF16)
    return h, (v - h.astype(F32)).astype(BF16)


def perm_map():
    m = np.zeros((64, 128), np.float32)
    for r in range(2):
        for c in range(4):
            for x in range(8):
                m[32 * r + 8 * c + x, 16 * c + 8 * r + x] = 1.0
    m[:, 64:] = m[:, :64]
    return m


def prep_targets(tpos, o_t, tag_dev, ta, xrow):
    lane8 = lax.broadcasted_iota(jnp.int32, (8, 128), 1)
    lane = lax.broadcasted_iota(jnp.int32, (8, 256), 1)
    sub = lax.broadcasted_iota(jnp.int32, (8, 256), 0)
    org = jnp.where(sub == 0, o_t[0], jnp.where(sub == 1, o_t[1], o_t[2]))
    jrow = lax.broadcasted_iota(jnp.int32, (64, 256), 0)
    jlane = lax.broadcasted_iota(jnp.int32, (64, 256), 1)
    for c in range(4):
        halves = []
        for t in range(2):
            v = jnp.zeros((8, 128), F32)
            for k in range(8):
                shift = (16 * (k - c)) % 128
                a = tpos[8 * t + k]
                if shift: a = pltpu.roll(a, shift, 1)
                v = jnp.where(lane8 // 16 == k, a, v)
            halves.append(v)
        raw = jnp.concatenate(halves, axis=1)
        delta = (c - 1.5) * SHIFT
        loc = (raw - org) * KAPPA - jnp.where(sub == 0, delta, 0.0)
        loc = jnp.where(sub < 3, loc, 0.0)
        xrow[c] = loc
        n2 = jnp.sum(loc * loc, axis=0, keepdims=True)
        v = jnp.where(sub == c, -2.0 * loc[0:1], jnp.where(sub == 4, -2.0 * loc[1:2], jnp.where(sub == 5, -2.0 * loc[2:3], jnp.where(sub == 6, n2, 0.0))))
        h, m, l = pieces(v)
        g6 = jnp.where((sub == c) | (sub == 4 + c), 1.0, 0.0)
        g7 = jnp.where(sub == c, 1.0, 0.0)
        tag = jnp.where((jlane // 16 == tag_dev) & (jrow == 16 * c + jlane % 16), HUGE, 0.0)
        ta[c] = jnp.concatenate([h, m, l, h, m, h, g6, g7, tag], axis=0).astype(BF16)


def prep_sources(src, slot, o_s, oy_r2, own_tag, emap, wmat, sb):
    low = lax.broadcasted_iota(jnp.int32, (8, 128), 1) < 64
    ra, rb = [], []
    for p in range(2):
        a, b = src[4 * slot + 2 * p], src[4 * slot + 2 * p + 1]
        ra.append(jnp.where(low, a, pltpu.roll(b, 64, 1)))
        rb.append(jnp.where(low, pltpu.roll(a, 64, 1), b))
    fa = jnp.concatenate(ra, axis=1)
    fb = jnp.concatenate(rb, axis=1)
    sub = lax.broadcasted_iota(jnp.int32, (8, 256), 0)
    org = jnp.where(sub == 0, o_s[0], jnp.where(sub == 1, o_s[1], o_s[2]))
    loc = (fa - org) * KAPPA
    yr2 = (fa[1:2] - oy_r2) * KAPPA
    f0 = jnp.where(sub < 3, loc, jnp.where(sub == 3, 1.0, fa))
    xs = [f0[k:k + 1] for k in range(3)]
    mom = [f0[4 + k:5 + k] for k in range(4)] + [fb[k:k + 1] for k in range(8)]
    us = []
    for d in range(2):
        for ri in range(2):
            b = d * 6 + ri * 3
            us.append(xs[0] * mom[b] + xs[1] * mom[b + 1] + xs[2] * mom[b + 2])
    f2 = jnp.concatenate(us + [jnp.zeros((4, 256), F32)], axis=0)
    feats = jnp.concatenate([f0, fb, f2, jnp.zeros((8, 256), F32)], axis=0)
    h, m, l = pieces(feats)
    frp = jnp.concatenate([h, m, l], axis=0).astype(BF16)
    for c in range(4):
        o = jnp.dot(emap[c], frp, preferred_element_type=F32)
        xe = o[:32]
        pr, pi = o[32:64] * xe, o[64:96] * xe
        ar, ai = o[96:128], o[128:160]
        for k, (re, im) in enumerate(((ar, ai), (pr, pi))):
            rh, rl = split(re); ih, il = split(im)
            wmat[c, :, pl.ds(512 * k, 256)] = jnp.concatenate([rh, ih, rl, il], axis=0)
            wmat[c, :, pl.ds(512 * k + 256, 256)] = jnp.concatenate([-ih, rh, -il, rl], axis=0)
    lane = lax.broadcasted_iota(jnp.int32, (64, 256), 1)
    j = lax.broadcasted_iota(jnp.int32, (64, 256), 0)
    tag = jnp.where(lane == own_tag + j, 1.0, 0.0)
    shift = (sub.astype(F32) - 1.5) * SHIFT
    va = jnp.where(sub < 4, xs[0] - shift, jnp.where(sub == 4, yr2, jnp.where(sub == 5, xs[2], jnp.where(sub == 6, 1.0, 0.0))))
    yz = yr2 * yr2 + xs[2] * xs[2]
    vb = jnp.where(sub < 4, va * va + yz, 0.0)
    ah, am, al = pieces(va); bh, bm, bl = pieces(vb)
    b6 = jnp.where(sub < 4, bh, pltpu.roll(bm, 4, 0))
    rows = jnp.concatenate([ah, ah, ah, am, am, al, b6, bl, tag], axis=0)
    sb[...] = jnp.concatenate([rows[:, :128].T, rows[:, 128:].T], axis=0).astype(BF16)


def finish(acc, xr, dy):
    t = acc[:64] + acc[64:]
    x = [xr[k:k + 1] for k in range(3)]
    x[1] = x[1] + dy
    out = [None] * 12
    for ri in range(2):
        row = lambda j: t[ri * 32 + 2 * j:ri * 32 + 2 * j + 2]
        s1 = [row(k) for k in range(3)]
        s2 = [[row(3 + 3 * a + k) for k in range(3)] for a in range(3)]
        s3 = [row(12 + k) for k in range(3)]
        inner = x[0] * s1[0] + x[1] * s1[1] + x[2] * s1[2] - (s2[0][0] + s2[1][1] + s2[2][2])
        for c in range(3):
            val = s3[c] + x[c] * inner - (x[0] * s2[c][0] + x[1] * s2[c][1] + x[2] * s2[c][2])
            for d in range(2):
                out[d * 6 + ri * 3 + c] = val[d:d + 1]
    return jnp.concatenate(out, axis=0)


def nn(a, b):
    return lax.dot_general(a, b, (((1,), (0,)), ((), ())), precision=lax.Precision.HIGHEST, preferred_element_type=F32)


def nt(a, b):
    return lax.dot_general(a, b, (((1,), (1,)), ((), ())), precision=lax.Precision.HIGHEST, preferred_element_type=F32)


def permuted(rows, table):
    h, m, l = pieces(rows)
    n = rows.shape[0]
    o = jnp.dot(jnp.concatenate([h, m, l], axis=0).astype(BF16), table, preferred_element_type=F32)
    return o[:n] + o[n : 2 * n] + o[2 * n :]


def kernel(pos_h, mom_h, ipr_h, ipi_h, mode_h, det_h, wid_h, emap_h, perm_h, unperm_h, out,
           pos, mom, ipr, ipi, mode, det, wid, emap, perm, unperm, in_sem,
           src, tgt, ta, xrow, wmat, sb, ga, gb, ra, rb, acc, amp, rs, zb, cb, ag, obuf, rbuf,
           tgt_s, tgt_r, src_s, src_r, fwd_s, fwd_r, rs_s, rs_r, zb_s, zb_r, cb_s, cb_r, ag_s, ag_r, o_s, o_r, pass_s, zf_s, zf_r, zfar):
    blk, grp = lax.axis_index("blk"), lax.axis_index("grp")
    zl, x, zh, y, core = blk // 4, blk % 4, grp // 8, (grp // 2) % 4, grp % 2
    me_r, me_z = x * 4 + y, zh * 8 + zl

    def at_r(r):
        return (zl * 4 + r // 4, zh * 8 + (r % 4) * 2 + core)

    def at_z(z):
        return ((z % 8) * 4 + x, (z // 8) * 8 + y * 2 + core)

    sibling = (blk, zh * 8 + y * 2 + (1 - core))

    barrier = pltpu.get_barrier_semaphore()

    def greet(s, _):
        pl.semaphore_signal(barrier, inc=1, device_id=at_r((me_r + s) % 16), device_id_type=MESH)
        return 0

    def greet_z(s, _):
        pl.semaphore_signal(barrier, inc=1, device_id=at_z(near(s)), device_id_type=MESH)
        return 0

    def near(s):
        return (me_z + 12 + s + s // 4) % 16

    lax.fori_loop(0, 8, greet_z, 0, unroll=4)
    lax.fori_loop(1, 16, greet, 0, unroll=5)
    pl.semaphore_signal(barrier, inc=1, device_id=sibling, device_id_type=MESH)

    fetched = [
        pltpu.make_async_copy(a, b, in_sem.at[k])
        for k, (a, b) in enumerate(
            zip(
                (pos_h, mom_h, perm_h, mode_h, emap_h, det_h, wid_h, ipr_h, ipi_h, unperm_h),
                (pos, mom, perm, mode, emap, det, wid, ipr, ipi, unperm),
            )
        )
    ]
    for copy in fetched:
        copy.start()

    mine = src.at[core]

    def remote(a, b, ss, rr, dev):
        return pltpu.make_async_remote_copy(src_ref=a, dst_ref=b, send_sem=ss, recv_sem=rr, device_id=dev, device_id_type=MESH)

    def spread_to(buf, ss, rr, me, where):
        def go(s, _):
            j = (me + s) % 16
            remote(buf.at[me], buf.at[me], ss.at[j], rr.at[me], where(j)).start()
            return 0
        lax.fori_loop(1, 16, go, 0, unroll=5)

    def arrived(buf, ss, rr, me, where):
        def go(s, _):
            j = (me + s) % 16
            remote(buf.at[j], buf.at[j], ss.at[j], rr.at[j], where(j)).wait_recv()
            return 0
        lax.fori_loop(1, 16, go, 0)

    def near_spread(buf, ss, rr):
        def go(s, _):
            z = near(s)
            remote(buf.at[me_z], buf.at[me_z], ss.at[z], rr.at[me_z], at_z(z)).start()
            return 0
        lax.fori_loop(0, 8, go, 0, unroll=4)

    def near_arrived(buf, ss, rr):
        def go(s, _):
            z = near(s)
            remote(buf.at[z], buf.at[z], ss.at[z], rr.at[z], at_z(z)).wait_recv()
            return 0
        lax.fori_loop(0, 8, go, 0)

    def near_sent(buf, ss, rr):
        def go(s, _):
            z = near(s)
            remote(buf.at[me_z], buf.at[me_z], ss.at[z], rr.at[me_z], at_z(z)).wait_send()
            return 0
        lax.fori_loop(0, 8, go, 0)

    up, down = (me_z + 4) % 16, (me_z + 12) % 16

    def passed(k):
        z = (me_z + jnp.where(k < 4, k + 1, 19 - k)) % 16
        to = jnp.where(k < 4, down, up)
        return remote(mine.at[z], mine.at[z], pass_s.at[k], src_r.at[z], at_z(to))

    def sent(buf, ss, rr, me, where):
        def go(s, _):
            j = (me + s) % 16
            remote(buf.at[me], buf.at[me], ss.at[j], rr.at[me], where(j)).wait_send()
            return 0
        lax.fori_loop(1, 16, go, 0)

    for copy in fetched[:3]:
        copy.wait()
    feats = jnp.concatenate(
        [pos[...], jnp.ones((1, 64), F32)]
        + [mom[d, c, ri : ri + 1] for d in range(2) for ri in range(2) for c in range(3)],
        axis=0,
    )
    moved = permuted(feats, perm[...])
    low = lax.broadcasted_iota(jnp.int32, (8, 128), 1) < 64
    tile = jnp.where(low, moved[:8], moved[8:])
    src[core, me_z] = tile
    tgt[me_r] = tile

    pl.semaphore_wait(barrier, 24)

    spread_to(tgt, tgt_s, tgt_r, me_r, at_r)
    near_spread(mine, src_s, src_r)

    fetched[3].wait()
    pa, pb = 0.0, 0.0
    for c in range(3):
        pc = jnp.concatenate([mom[d, c] for d in range(2)], axis=0)
        pa = pa + nn(pc, mode[0, c])
        pb = pb + nn(pc, mode[1, c])
    for d in range(2):
        re = pa[2 * d : 2 * d + 1] - pb[2 * d + 1 : 2 * d + 2]
        im = pa[2 * d + 1 : 2 * d + 2] + pb[2 * d : 2 * d + 1]
        for q in range(4):
            amp[8 * d + q] = re[:, 128 * q : 128 * q + 128]
            amp[8 * d + 4 + q] = im[:, 128 * q : 128 * q + 128]
    for copy in fetched[4:]:
        copy.wait()

    def scatter(s, _):
        j = (me_r + s) % 16
        remote(amp.at[j], rs.at[me_r], rs_s.at[j], rs_r.at[me_r], at_r(j)).start()
        return 0

    lax.fori_loop(1, 16, scatter, 0, unroll=5)
    rs[me_r] = amp[me_r]

    ox, oz, oyt = 15.5, 4.0 * zl.astype(F32) + 1.5, (16 * zh + 2 * core).astype(F32) + 6.5
    near_arrived(mine, src_s, src_r)

    def pass_on(k, _):
        passed(k).start()
        return 0

    lax.fori_loop(0, 7, pass_on, 0)
    arrived(tgt, tgt_s, tgt_r, me_r, at_r)
    prep_targets(tgt, (ox, oyt, oz), me_r, ta, xrow)
    acc[...] = jnp.zeros_like(acc)
    gb[...] = jnp.zeros_like(gb)
    wmat[1, 3] = jnp.zeros((128, 1024), BF16)

    def stage(w, gold, gnew, rnow, nxt, rnext):
        total = None
        for q in range(8):
            ko = 256 * (q % 4)
            part = jnp.dot(w[:, ko : ko + 256], gold[q // 4, ko : ko + 256], preferred_element_type=F32)
            if nxt is not None and q % 4 == 0:
                top = 32 * q
                r2 = jnp.dot(sb[top : top + 128], ta[nxt], preferred_element_type=F32)
            for k in (2 * q, 2 * q + 1):
                for n, v in enumerate(planes(rnow[16 * k : 16 * k + 16, :])):
                    h, l = split(v)
                    gnew[0, 256 * n + 16 * k : 256 * n + 16 * k + 16, :] = h
                    gnew[1, 256 * n + 16 * k : 256 * n + 16 * k + 16, :] = l
            if nxt is not None and q % 4 == 0:
                rnext[top : top + 128] = r2
            total = part if total is None else total + part
        return total

    def one_block(step, _):
        quad = (me_z // 4 + step // 2) % 4
        away = step % 2
        from_core = (core + away) % 2
        quad_ref = src.at[from_core, pl.ds(4 * quad, 4)]

        @pl.when(away == 0)
        def _():
            def go(k, _):
                z = 4 * quad + k
                gap = (z + 20 - me_z) % 16
                @pl.when(gap > 8)
                def _():
                    remote(mine.at[z], mine.at[z], src_s.at[z], src_r.at[z], at_z(z)).wait_recv()
                return 0
            lax.fori_loop(0, 4, go, 0)
            remote(quad_ref, quad_ref, fwd_s.at[quad], fwd_r.at[quad], sibling).start()

        @pl.when(away == 1)
        def _():
            remote(quad_ref, quad_ref, fwd_s.at[quad], fwd_r.at[quad], sibling).wait_recv()

        half = quad // 2
        oys = (16 * half + 4 * y).astype(F32) + 1.5
        own = jnp.where(step == 0, (me_z % 4) * 64, -1000)
        par = step % 2
        prep_sources(src.at[from_core], quad, (ox, oys, oz), oyt, own, emap, wmat.at[par], sb)
        ra[...] = jnp.dot(sb[...], ta[0], preferred_element_type=F32)
        before = ((me_z // 4 + (step + 7) // 2) % 4) // 2
        acc[before, 3] += stage(wmat.at[1 - par, 3], gb, ga, ra, 1, rb)
        acc[half, 0] += stage(wmat.at[par, 0], ga, gb, rb, 2, ra)
        acc[half, 1] += stage(wmat.at[par, 1], gb, ga, ra, 3, rb)
        acc[half, 2] += stage(wmat.at[par, 2], ga, gb, rb, None, None)

        @pl.when(step == 1)
        def _():
            arrived(rs, rs_s, rs_r, me_r, at_r)
            zb[me_z] = jnp.sum(rs[...], axis=0)
            near_spread(zb, zb_s, zb_r)

        @pl.when(step == 3)
        def _():
            near_arrived(zb, zb_s, zb_r)
            above = zb[(me_z + 1) % 16] + zb[(me_z + 2) % 16] + zb[(me_z + 3) % 16]
            above = above + zb[up]
            below = zb[(me_z + 15) % 16] + zb[(me_z + 14) % 16] + zb[(me_z + 13) % 16]
            zfar[0] = above
            zfar[1] = below
            zfar[4] = above + below + zb[down] + zb[me_z]
            remote(zfar.at[0], zfar.at[2], zf_s.at[0], zf_r.at[0], at_z(down)).start()
            remote(zfar.at[1], zfar.at[3], zf_s.at[1], zf_r.at[1], at_z(up)).start()

        @pl.when(step == 5)
        def _():
            remote(zfar.at[0], zfar.at[2], zf_s.at[0], zf_r.at[0], at_z(up)).wait_recv()
            remote(zfar.at[1], zfar.at[3], zf_s.at[1], zf_r.at[1], at_z(down)).wait_recv()
            cb[core] = zfar[2] + zfar[3] + zfar[4]
            remote(cb.at[core], cb.at[core], cb_s.at[0], cb_r.at[0], sibling).start()

        @pl.when(step == 6)
        def _():
            remote(cb.at[1 - core], cb.at[1 - core], cb_s.at[0], cb_r.at[0], sibling).wait_recv()
            ag[me_r] = cb[0] + cb[1]
            spread_to(ag, ag_s, ag_r, me_r, at_r)

        return 0

    lax.fori_loop(0, 8, one_block, 0)
    last = ((me_z // 4 + 3) % 4) // 2
    w = wmat[1, 3]
    acc[last, 3] += jnp.dot(w, gb[0], preferred_element_type=F32) + jnp.dot(w, gb[1], preferred_element_type=F32)

    lane = lax.broadcasted_iota(jnp.int32, (8, 128), 1)
    fa, fb = [], []
    for c in range(4):
        f = 0.0
        for half in range(2):
            dy = (oyt - ((16 * half + 4 * y).astype(F32) + 1.5)) * KAPPA
            f = f + finish(acc[half, c], xrow[c], dy)
        fa.append(f[:8])
        fb.append(jnp.concatenate([f[8:], jnp.zeros((4, 256), F32)], axis=0))
    for r in range(16):
        t, k = r // 8, r % 8
        v = jnp.zeros((8, 128), F32)
        for c in range(4):
            for top, rows in ((0, fa[c]), (64, fb[c])):
                a = rows[:, 128 * t : 128 * t + 128]
                shift = (top + 16 * (c - k)) % 128
                if shift:
                    a = pltpu.roll(a, shift, 1)
                v = jnp.where(lane // 16 == top // 16 + c, a, v)
        obuf[r] = v

    def give(s, _):
        j = (me_r + s) % 16
        remote(obuf.at[j], rbuf.at[me_r], o_s.at[j], o_r.at[me_r], at_r(j)).start()
        return 0

    lax.fori_loop(1, 16, give, 0, unroll=5)
    rbuf[me_r] = obuf[me_r]

    arrived(ag, ag_s, ag_r, me_r, at_r)
    rows = [jnp.concatenate([ag[4 * k + q] for q in range(4)], axis=1) for k in range(4)]
    den = det[...] * det[...] + wid[...] * wid[...]
    rr, ri = det[...] / den, wid[...] / den
    weighted = []
    for d in range(2):
        re, im = rows[2 * d], rows[2 * d + 1]
        weighted += [rr * re - ri * im, rr * im + ri * re]
    weighted = jnp.concatenate(weighted, axis=0)
    part = []
    for c in range(3):
        part.append((nt(weighted, mode[0, c]), nt(weighted, mode[1, c])))

    sent(tgt, tgt_s, tgt_r, me_r, at_r)
    near_sent(mine, src_s, src_r)
    near_sent(zb, zb_s, zb_r)

    def pass_done(k, _):
        passed(k).wait_send()
        return 0

    lax.fori_loop(0, 7, pass_done, 0)
    remote(zfar.at[0], zfar.at[2], zf_s.at[0], zf_r.at[0], at_z(down)).wait_send()
    remote(zfar.at[1], zfar.at[3], zf_s.at[1], zf_r.at[1], at_z(up)).wait_send()
    sent(ag, ag_s, ag_r, me_r, at_r)

    def settle(s, _):
        j = (me_r + s) % 16
        remote(amp.at[j], rs.at[me_r], rs_s.at[j], rs_r.at[me_r], at_r(j)).wait_send()
        remote(obuf.at[j], rbuf.at[me_r], o_s.at[j], o_r.at[me_r], at_r(j)).wait_send()
        return 0

    lax.fori_loop(1, 16, settle, 0)
    remote(cb.at[core], cb.at[core], cb_s.at[0], cb_r.at[0], sibling).wait_send()

    def settle_quads(q, _):
        quad_ref = mine.at[pl.ds(4 * q, 4)]
        remote(quad_ref, quad_ref, fwd_s.at[q], fwd_r.at[q], sibling).wait_send()
        return 0

    lax.fori_loop(0, 4, settle_quads, 0)
    arrived(rbuf, o_s, o_r, me_r, at_r)
    total = jnp.sum(rbuf[...], axis=0)
    total = jnp.concatenate([total, pltpu.roll(total, 64, 1)], axis=0)[:, :64]
    field = permuted(total, unperm[...]) * (COUPLING * KAPPA)
    pr, pi = ipr[...], ipi[...]
    for d in range(2):
        for c in range(3):
            a, b = part[c]
            pre, pim = mom[d, c, 0:1], mom[d, c, 1:2]
            k = 6 * d + c
            mre = a[2 * d : 2 * d + 1] - b[2 * d + 1 : 2 * d + 2]
            mim = a[2 * d + 1 : 2 * d + 2] + b[2 * d : 2 * d + 1]
            out[d, c, 0:1] = pr * pre - pi * pim - field[k : k + 1, :64] - mre
            out[d, c, 1:2] = pr * pim + pi * pre - field[k + 3 : k + 4, :64] - mim


def on_device(positions, moments, inv_polar_re, inv_polar_im, mode_field, mode_detune, mode_width):
    table = perm_map()
    back = np.zeros((64, 128), np.float32)
    back[:, :64] = table[:, :64].T
    vm = pl.BlockSpec(memory_space=pltpu.VMEM)
    dma = lambda n: pltpu.SemaphoreType.DMA((n,))
    arrays = (
        positions,
        moments.transpose(0, 2, 1, 3),
        inv_polar_re.reshape(1, -1),
        inv_polar_im.reshape(1, -1),
        mode_field,
        mode_detune.reshape(1, -1),
        mode_width.reshape(1, -1),
        jnp.asarray(feature_maps(), BF16),
        jnp.asarray(table, BF16),
        jnp.asarray(back, BF16),
    )
    response = pl.pallas_call(
        kernel,
        out_shape=jax.ShapeDtypeStruct(arrays[1].shape, F32),
        in_specs=[pl.BlockSpec(memory_space=pl.ANY)] * 10,
        out_specs=vm,
        scratch_shapes=[pltpu.VMEM(a.shape, a.dtype) for a in arrays]
        + [
            dma(10),
            pltpu.VMEM((2, 16, 8, 128), F32),
            pltpu.VMEM((16, 8, 128), F32),
            pltpu.VMEM((4, 128, 256), BF16),
            pltpu.VMEM((4, 8, 256), F32),
            pltpu.VMEM((2, 4, 128, 1024), BF16),
            pltpu.VMEM((256, 128), BF16),
            pltpu.VMEM((2, 1024, 256), BF16),
            pltpu.VMEM((2, 1024, 256), BF16),
            pltpu.VMEM((256, 256), F32),
            pltpu.VMEM((256, 256), F32),
            pltpu.VMEM((2, 4, 128, 256), F32),
            pltpu.VMEM((16, 1, 128), F32),
            pltpu.VMEM((16, 1, 128), F32),
            pltpu.VMEM((16, 1, 128), F32),
            pltpu.VMEM((2, 1, 128), F32),
            pltpu.VMEM((16, 1, 128), F32),
            pltpu.VMEM((16, 8, 128), F32),
            pltpu.VMEM((16, 8, 128), F32),
        ]
        + [dma(16), dma(16), dma(16), dma(16), dma(4), dma(4), dma(16), dma(16)]
        + [dma(16), dma(16), dma(1), dma(1), dma(16), dma(16), dma(16), dma(16)]
        + [dma(7), dma(2), dma(2), pltpu.VMEM((5, 1, 128), F32)],
        compiler_params=pltpu.CompilerParams(collective_id=0, has_side_effects=True, vmem_limit_bytes=60 << 20),
    )(*arrays)
    return response.transpose(0, 2, 1, 3)


def solution(mesh):
    both = ("blk", "grp")
    placed = (P(None, both), P(None, None, None, both), P(both), P(both), P(None, None, both, None), P(), P())
    return jax.shard_map(on_device, mesh=mesh, in_specs=placed, out_specs=P(None, None, None, both), check_vma=False)
```

```python
import math

import jax
import jax.numpy as jnp
import numpy as np
from jax import lax
from jax.experimental import pallas as pl
from jax.experimental.pallas import tpu as pltpu
from jax.sharding import PartitionSpec as P

F32, BF16 = jnp.float32, jnp.bfloat16
MESH = pl.DeviceIdType.MESH
KAPPA = 1.0 / (2.0 * math.pi)
COUPLING = 0.05
SHIFT = 1.25
HUGE = 1e30


def feature_maps():
    e = np.zeros((4, 160, 96), np.float32)
    for c in range(4):
        delta = (c - 1.5) * SHIFT
        base = np.zeros((160, 32), np.float32)
        for d in range(2):
            for j in range(15):
                row = j * 2 + d
                if j < 3:
                    base[row, 3] = 1.0; comp = j
                elif j < 12:
                    a, comp = divmod(j - 3, 3)
                else:
                    a, comp = j - 12, None
                if j >= 3:
                    base[row, a] = 1.0
                    if a == 0: base[row, 3] = -delta
                for ri in range(2):
                    m = 4 + d * 6 + ri * 3
                    if comp is not None:
                        base[32 + 32 * ri + row, m + comp] = -3.0
                    else:
                        base[32 + 32 * ri + row, 16 + d * 2 + ri] = -3.0
                        base[32 + 32 * ri + row, m] = 3.0 * delta
                        base[96 + 32 * ri + row, m + a] = 1.0
        for piece in range(3):
            e[c, :, 32 * piece:32 * piece + 32] = base
    return e


def pieces(v):
    h = v.astype(BF16).astype(F32)
    rest = v - h
    m = rest.astype(BF16).astype(F32)
    return h, m, rest - m


S4 = [4.442867982147176, -7.307445408741119, 3.59480206222511, -0.7844035161415288]
C5 = [1.4142134965690698, -6.978850988398392, 5.73946117217025, -1.8835629909695983, 0.3106981907767927]

def planes(r2):
    y = lax.rsqrt(r2)
    w = r2 * y
    f = w - jnp.round(w)
    t = f * f
    s = S4[-1]
    for k in S4[-2::-1]: s = s * t + k
    s = s * f
    c = C5[-1]
    for k in C5[-2::-1]: c = c * t + k
    y23 = y * (2.0 / 3.0)
    sy = s * y23
    gr = y23 - s * sy
    gi = sy * c
    q = y * y
    u = y * (1.5 * KAPPA)
    v1 = 1.5 - q * (1.5 * KAPPA * KAPPA)
    ar = gr * v1 - gi * u
    ai = gi * v1 + gr * u
    br = q * (ar - gr)
    bi = q * (ai - gi)
    return ar, ai, br, bi


def split(v):
    h = v.astype(BF16)
    return h, (v - h.astype(F32)).astype(BF16)


def perm_map():
    m = np.zeros((64, 128), np.float32)
    for r in range(2):
        for c in range(4):
            for x in range(8):
                m[32 * r + 8 * c + x, 16 * c + 8 * r + x] = 1.0
    m[:, 64:] = m[:, :64]
    return m


def prep_targets(tpos, o_t, tag_dev, ta, xrow):
    lane8 = lax.broadcasted_iota(jnp.int32, (8, 128), 1)
    lane = lax.broadcasted_iota(jnp.int32, (8, 256), 1)
    sub = lax.broadcasted_iota(jnp.int32, (8, 256), 0)
    org = jnp.where(sub == 0, o_t[0], jnp.where(sub == 1, o_t[1], o_t[2]))
    jrow = lax.broadcasted_iota(jnp.int32, (64, 256), 0)
    jlane = lax.broadcasted_iota(jnp.int32, (64, 256), 1)
    for c in range(4):
        halves = []
        for t in range(2):
            v = jnp.zeros((8, 128), F32)
            for k in range(8):
                shift = (16 * (k - c)) % 128
                a = tpos[8 * t + k]
                if shift: a = pltpu.roll(a, shift, 1)
                v = jnp.where(lane8 // 16 == k, a, v)
            halves.append(v)
        raw = jnp.concatenate(halves, axis=1)
        delta = (c - 1.5) * SHIFT
        loc = (raw - org) * KAPPA - jnp.where(sub == 0, delta, 0.0)
        loc = jnp.where(sub < 3, loc, 0.0)
        xrow[c] = loc
        n2 = jnp.sum(loc * loc, axis=0, keepdims=True)
        v = jnp.where(sub == c, -2.0 * loc[0:1], jnp.where(sub == 4, -2.0 * loc[1:2], jnp.where(sub == 5, -2.0 * loc[2:3], jnp.where(sub == 6, n2, 0.0))))
        h, m, l = pieces(v)
        g6 = jnp.where((sub == c) | (sub == 4 + c), 1.0, 0.0)
        g7 = jnp.where(sub == c, 1.0, 0.0)
        tag = jnp.where((jlane // 16 == tag_dev) & (jrow == 16 * c + jlane % 16), HUGE, 0.0)
        ta[c] = jnp.concatenate([h, m, l, h, m, h, g6, g7, tag], axis=0).astype(BF16)


def prep_sources(src, slot, o_s, oy_r2, own_tag, emap, wmat, sb):
    low = lax.broadcasted_iota(jnp.int32, (8, 128), 1) < 64
    ra, rb = [], []
    for p in range(2):
        a, b = src[4 * slot + 2 * p], src[4 * slot + 2 * p + 1]
        ra.append(jnp.where(low, a, pltpu.roll(b, 64, 1)))
        rb.append(jnp.where(low, pltpu.roll(a, 64, 1), b))
    fa = jnp.concatenate(ra, axis=1)
    fb = jnp.concatenate(rb, axis=1)
    sub = lax.broadcasted_iota(jnp.int32, (8, 256), 0)
    org = jnp.where(sub == 0, o_s[0], jnp.where(sub == 1, o_s[1], o_s[2]))
    loc = (fa - org) * KAPPA
    yr2 = (fa[1:2] - oy_r2) * KAPPA
    f0 = jnp.where(sub < 3, loc, jnp.where(sub == 3, 1.0, fa))
    xs = [f0[k:k + 1] for k in range(3)]
    mom = [f0[4 + k:5 + k] for k in range(4)] + [fb[k:k + 1] for k in range(8)]
    us = []
    for d in range(2):
        for ri in range(2):
            b = d * 6 + ri * 3
            us.append(xs[0] * mom[b] + xs[1] * mom[b + 1] + xs[2] * mom[b + 2])
    f2 = jnp.concatenate(us + [jnp.zeros((4, 256), F32)], axis=0)
    feats = jnp.concatenate([f0, fb, f2, jnp.zeros((8, 256), F32)], axis=0)
    h, m, l = pieces(feats)
    frp = jnp.concatenate([h, m, l], axis=0).astype(BF16)
    for c in range(4):
        o = jnp.dot(emap[c], frp, preferred_element_type=F32)
        xe = o[:32]
        pr, pi = o[32:64] * xe, o[64:96] * xe
        ar, ai = o[96:128], o[128:160]
        for k, (re, im) in enumerate(((ar, ai), (pr, pi))):
            rh, rl = split(re); ih, il = split(im)
            wmat[c, :, pl.ds(512 * k, 256)] = jnp.concatenate([rh, ih, rl, il], axis=0)
            wmat[c, :, pl.ds(512 * k + 256, 256)] = jnp.concatenate([-ih, rh, -il, rl], axis=0)
    lane = lax.broadcasted_iota(jnp.int32, (64, 256), 1)
    j = lax.broadcasted_iota(jnp.int32, (64, 256), 0)
    tag = jnp.where(lane == own_tag + j, 1.0, 0.0)
    shift = (sub.astype(F32) - 1.5) * SHIFT
    va = jnp.where(sub < 4, xs[0] - shift, jnp.where(sub == 4, yr2, jnp.where(sub == 5, xs[2], jnp.where(sub == 6, 1.0, 0.0))))
    yz = yr2 * yr2 + xs[2] * xs[2]
    vb = jnp.where(sub < 4, va * va + yz, 0.0)
    ah, am, al = pieces(va); bh, bm, bl = pieces(vb)
    b6 = jnp.where(sub < 4, bh, pltpu.roll(bm, 4, 0))
    rows = jnp.concatenate([ah, ah, ah, am, am, al, b6, bl, tag], axis=0)
    sb[...] = jnp.concatenate([rows[:, :128].T, rows[:, 128:].T], axis=0).astype(BF16)


def finish(acc, xr, dy):
    t = acc[:64] + acc[64:]
    x = [xr[k:k + 1] for k in range(3)]
    x[1] = x[1] + dy
    out = [None] * 12
    for ri in range(2):
        row = lambda j: t[ri * 32 + 2 * j:ri * 32 + 2 * j + 2]
        s1 = [row(k) for k in range(3)]
        s2 = [[row(3 + 3 * a + k) for k in range(3)] for a in range(3)]
        s3 = [row(12 + k) for k in range(3)]
        inner = x[0] * s1[0] + x[1] * s1[1] + x[2] * s1[2] - (s2[0][0] + s2[1][1] + s2[2][2])
        for c in range(3):
            val = s3[c] + x[c] * inner - (x[0] * s2[c][0] + x[1] * s2[c][1] + x[2] * s2[c][2])
            for d in range(2):
                out[d * 6 + ri * 3 + c] = val[d:d + 1]
    return jnp.concatenate(out, axis=0)


def nn(a, b):
    return lax.dot_general(a, b, (((1,), (0,)), ((), ())), precision=lax.Precision.HIGHEST, preferred_element_type=F32)


def nt(a, b):
    return lax.dot_general(a, b, (((1,), (1,)), ((), ())), precision=lax.Precision.HIGHEST, preferred_element_type=F32)


def permuted(rows, table):
    h, m, l = pieces(rows)
    n = rows.shape[0]
    o = jnp.dot(jnp.concatenate([h, m, l], axis=0).astype(BF16), table, preferred_element_type=F32)
    return o[:n] + o[n : 2 * n] + o[2 * n :]


def kernel(pos_h, mom_h, ipr_h, ipi_h, mode_h, det_h, wid_h, emap_h, perm_h, unperm_h, out,
           pos, mom, ipr, ipi, mode, det, wid, emap, perm, unperm, in_sem,
           src, tgt, ta, xrow, wmat, sb, ga, gb, ra, rb, acc, amp, rs, zb, cb, ag, obuf, rbuf,
           tgt_s, tgt_r, src_s, src_r, fwd_s, fwd_r, rs_s, rs_r, zb_s, zb_r, cb_s, cb_r, ag_s, ag_r, o_s, o_r, pass_s, zf_s, zf_r, zfar):
    blk, grp = lax.axis_index("blk"), lax.axis_index("grp")
    zl, x, zh, y, core = blk // 4, blk % 4, grp // 8, (grp // 2) % 4, grp % 2
    me_r, me_z = x * 4 + y, zh * 8 + zl

    def at_r(r):
        return (zl * 4 + r // 4, zh * 8 + (r % 4) * 2 + core)

    def at_z(z):
        return ((z % 8) * 4 + x, (z // 8) * 8 + y * 2 + core)

    sibling = (blk, zh * 8 + y * 2 + (1 - core))

    fetched = [
        pltpu.make_async_copy(a, b, in_sem.at[k])
        for k, (a, b) in enumerate(
            zip(
                (pos_h, mom_h, perm_h, mode_h, emap_h, det_h, wid_h, ipr_h, ipi_h, unperm_h),
                (pos, mom, perm, mode, emap, det, wid, ipr, ipi, unperm),
            )
        )
    ]
    for copy in fetched:
        copy.start()

    barrier = pltpu.get_barrier_semaphore()

    def greet(s, _):
        pl.semaphore_signal(barrier, inc=1, device_id=at_r((me_r + s) % 16), device_id_type=MESH)
        return 0

    def greet_z(s, _):
        pl.semaphore_signal(barrier, inc=1, device_id=at_z(near(s)), device_id_type=MESH)
        return 0

    def near(s):
        return (me_z + 12 + s + s // 4) % 16

    lax.fori_loop(0, 8, greet_z, 0, unroll=4)
    lax.fori_loop(1, 16, greet, 0, unroll=5)
    pl.semaphore_signal(barrier, inc=1, device_id=sibling, device_id_type=MESH)


    mine = src.at[core]

    def remote(a, b, ss, rr, dev):
        return pltpu.make_async_remote_copy(src_ref=a, dst_ref=b, send_sem=ss, recv_sem=rr, device_id=dev, device_id_type=MESH)

    def spread_to(buf, ss, rr, me, where):
        def go(s, _):
            j = (me + s) % 16
            remote(buf.at[me], buf.at[me], ss.at[0], rr.at[0], where(j)).start()
            return 0
        lax.fori_loop(1, 16, go, 0, unroll=5)

    def arrived(buf, ss, rr, me, where):
        many = buf.at[pl.ds(0, 15)]
        remote(many, many, ss.at[0], rr.at[0], where((me + 1) % 16)).wait_recv()

    def near_spread(buf, ss, rr):
        def go(s, _):
            z = near(s)
            remote(buf.at[me_z], buf.at[me_z], ss.at[z], rr.at[me_z], at_z(z)).start()
            return 0
        lax.fori_loop(0, 8, go, 0, unroll=4)

    def near_arrived(buf, ss, rr):
        def go(s, _):
            z = near(s)
            remote(buf.at[z], buf.at[z], ss.at[z], rr.at[z], at_z(z)).wait_recv()
            return 0
        lax.fori_loop(0, 8, go, 0)

    def near_sent(buf, ss, rr):
        def go(s, _):
            z = near(s)
            remote(buf.at[me_z], buf.at[me_z], ss.at[z], rr.at[me_z], at_z(z)).wait_send()
            return 0
        lax.fori_loop(0, 8, go, 0)

    up, down = (me_z + 4) % 16, (me_z + 12) % 16

    def passed(k):
        z = (me_z + jnp.where(k < 4, k + 1, 19 - k)) % 16
        to = jnp.where(k < 4, down, up)
        return remote(mine.at[z], mine.at[z], pass_s.at[k], src_r.at[z], at_z(to))

    def sent(buf, ss, rr, me, where):
        many = buf.at[pl.ds(0, 15)]
        remote(many, many, ss.at[0], rr.at[0], where((me + 1) % 16)).wait_send()

    for copy in fetched[:3]:
        copy.wait()
    feats = jnp.concatenate(
        [pos[...], jnp.ones((1, 64), F32)]
        + [mom[d, c, ri : ri + 1] for d in range(2) for ri in range(2) for c in range(3)],
        axis=0,
    )
    moved = permuted(feats, perm[...])
    low = lax.broadcasted_iota(jnp.int32, (8, 128), 1) < 64
    tile = jnp.where(low, moved[:8], moved[8:])
    src[core, me_z] = tile
    tgt[me_r] = tile

    pl.semaphore_wait(barrier, 24)

    spread_to(tgt, tgt_s, tgt_r, me_r, at_r)
    near_spread(mine, src_s, src_r)

    fetched[3].wait()
    pa, pb = 0.0, 0.0
    for c in range(3):
        pc = jnp.concatenate([mom[d, c] for d in range(2)], axis=0)
        pa = pa + nn(pc, mode[0, c])
        pb = pb + nn(pc, mode[1, c])
    for d in range(2):
        re = pa[2 * d : 2 * d + 1] - pb[2 * d + 1 : 2 * d + 2]
        im = pa[2 * d + 1 : 2 * d + 2] + pb[2 * d : 2 * d + 1]
        for q in range(4):
            amp[8 * d + q] = re[:, 128 * q : 128 * q + 128]
            amp[8 * d + 4 + q] = im[:, 128 * q : 128 * q + 128]
    for copy in fetched[4:]:
        copy.wait()

    def scatter(s, _):
        j = (me_r + s) % 16
        remote(amp.at[j], rs.at[me_r], rs_s.at[0], rs_r.at[0], at_r(j)).start()
        return 0

    lax.fori_loop(1, 16, scatter, 0, unroll=5)
    rs[me_r] = amp[me_r]

    ox, oz, oyt = 15.5, 4.0 * zl.astype(F32) + 1.5, (16 * zh + 2 * core).astype(F32) + 6.5
    near_arrived(mine, src_s, src_r)

    def pass_on(k, _):
        passed(k).start()
        return 0

    lax.fori_loop(0, 7, pass_on, 0)
    arrived(tgt, tgt_s, tgt_r, me_r, at_r)
    prep_targets(tgt, (ox, oyt, oz), me_r, ta, xrow)
    acc[...] = jnp.zeros_like(acc)
    gb[...] = jnp.zeros_like(gb)
    wmat[1, 3] = jnp.zeros((128, 1024), BF16)

    def stage(w, gold, gnew, rnow, nxt, rnext):
        total = None
        for q in range(8):
            ko = 256 * (q % 4)
            part = jnp.dot(w[:, ko : ko + 256], gold[q // 4, ko : ko + 256], preferred_element_type=F32)
            if nxt is not None and q % 4 == 0:
                top = 32 * q
                r2 = jnp.dot(sb[top : top + 128], ta[nxt], preferred_element_type=F32)
            for k in (2 * q, 2 * q + 1):
                for n, v in enumerate(planes(rnow[16 * k : 16 * k + 16, :])):
                    h, l = split(v)
                    gnew[0, 256 * n + 16 * k : 256 * n + 16 * k + 16, :] = h
                    gnew[1, 256 * n + 16 * k : 256 * n + 16 * k + 16, :] = l
            if nxt is not None and q % 4 == 0:
                rnext[top : top + 128] = r2
            total = part if total is None else total + part
        return total

    def one_block(step, _):
        quad = (me_z // 4 + step // 2) % 4
        away = step % 2
        from_core = (core + away) % 2
        quad_ref = src.at[from_core, pl.ds(4 * quad, 4)]

        @pl.when(away == 0)
        def _():
            def go(k, _):
                z = 4 * quad + k
                gap = (z + 20 - me_z) % 16
                @pl.when(gap > 8)
                def _():
                    remote(mine.at[z], mine.at[z], src_s.at[z], src_r.at[z], at_z(z)).wait_recv()
                return 0
            lax.fori_loop(0, 4, go, 0)
            remote(quad_ref, quad_ref, fwd_s.at[quad], fwd_r.at[quad], sibling).start()

        @pl.when(away == 1)
        def _():
            remote(quad_ref, quad_ref, fwd_s.at[quad], fwd_r.at[quad], sibling).wait_recv()

        half = quad // 2
        oys = (16 * half + 4 * y).astype(F32) + 1.5
        own = jnp.where(step == 0, (me_z % 4) * 64, -1000)
        par = step % 2
        prep_sources(src.at[from_core], quad, (ox, oys, oz), oyt, own, emap, wmat.at[par], sb)
        ra[...] = jnp.dot(sb[...], ta[0], preferred_element_type=F32)
        before = ((me_z // 4 + (step + 7) // 2) % 4) // 2
        acc[before, 3] += stage(wmat.at[1 - par, 3], gb, ga, ra, 1, rb)
        acc[half, 0] += stage(wmat.at[par, 0], ga, gb, rb, 2, ra)
        acc[half, 1] += stage(wmat.at[par, 1], gb, ga, ra, 3, rb)
        acc[half, 2] += stage(wmat.at[par, 2], ga, gb, rb, None, None)

        @pl.when(step == 1)
        def _():
            arrived(rs, rs_s, rs_r, me_r, at_r)
            zb[me_z] = jnp.sum(rs[...], axis=0)
            near_spread(zb, zb_s, zb_r)

        @pl.when(step == 3)
        def _():
            near_arrived(zb, zb_s, zb_r)
            above = zb[(me_z + 1) % 16] + zb[(me_z + 2) % 16] + zb[(me_z + 3) % 16]
            above = above + zb[up]
            below = zb[(me_z + 15) % 16] + zb[(me_z + 14) % 16] + zb[(me_z + 13) % 16]
            zfar[0] = above
            zfar[1] = below
            zfar[4] = above + below + zb[down] + zb[me_z]
            remote(zfar.at[0], zfar.at[2], zf_s.at[0], zf_r.at[0], at_z(down)).start()
            remote(zfar.at[1], zfar.at[3], zf_s.at[1], zf_r.at[1], at_z(up)).start()

        @pl.when(step == 5)
        def _():
            remote(zfar.at[0], zfar.at[2], zf_s.at[0], zf_r.at[0], at_z(up)).wait_recv()
            remote(zfar.at[1], zfar.at[3], zf_s.at[1], zf_r.at[1], at_z(down)).wait_recv()
            cb[core] = zfar[2] + zfar[3] + zfar[4]
            remote(cb.at[core], cb.at[core], cb_s.at[0], cb_r.at[0], sibling).start()

        @pl.when(step == 6)
        def _():
            remote(cb.at[1 - core], cb.at[1 - core], cb_s.at[0], cb_r.at[0], sibling).wait_recv()
            ag[me_r] = cb[0] + cb[1]
            spread_to(ag, ag_s, ag_r, me_r, at_r)

        return 0

    lax.fori_loop(0, 8, one_block, 0)
    last = ((me_z // 4 + 3) % 4) // 2
    w = wmat[1, 3]
    acc[last, 3] += jnp.dot(w, gb[0], preferred_element_type=F32) + jnp.dot(w, gb[1], preferred_element_type=F32)

    lane = lax.broadcasted_iota(jnp.int32, (8, 128), 1)
    fa, fb = [], []
    for c in range(4):
        f = 0.0
        for half in range(2):
            dy = (oyt - ((16 * half + 4 * y).astype(F32) + 1.5)) * KAPPA
            f = f + finish(acc[half, c], xrow[c], dy)
        fa.append(f[:8])
        fb.append(jnp.concatenate([f[8:], jnp.zeros((4, 256), F32)], axis=0))
    for r in range(16):
        t, k = r // 8, r % 8
        v = jnp.zeros((8, 128), F32)
        for c in range(4):
            for top, rows in ((0, fa[c]), (64, fb[c])):
                a = rows[:, 128 * t : 128 * t + 128]
                shift = (top + 16 * (c - k)) % 128
                if shift:
                    a = pltpu.roll(a, shift, 1)
                v = jnp.where(lane // 16 == top // 16 + c, a, v)
        obuf[r] = v

    def give(s, _):
        j = (me_r + s) % 16
        remote(obuf.at[j], rbuf.at[me_r], o_s.at[0], o_r.at[0], at_r(j)).start()
        return 0

    lax.fori_loop(1, 16, give, 0, unroll=5)
    rbuf[me_r] = obuf[me_r]

    arrived(ag, ag_s, ag_r, me_r, at_r)
    rows = [jnp.concatenate([ag[4 * k + q] for q in range(4)], axis=1) for k in range(4)]
    den = det[...] * det[...] + wid[...] * wid[...]
    rr, ri = det[...] / den, wid[...] / den
    weighted = []
    for d in range(2):
        re, im = rows[2 * d], rows[2 * d + 1]
        weighted += [rr * re - ri * im, rr * im + ri * re]
    weighted = jnp.concatenate(weighted, axis=0)
    part = []
    for c in range(3):
        part.append((nt(weighted, mode[0, c]), nt(weighted, mode[1, c])))

    sent(tgt, tgt_s, tgt_r, me_r, at_r)
    near_sent(mine, src_s, src_r)
    near_sent(zb, zb_s, zb_r)

    def pass_done(k, _):
        passed(k).wait_send()
        return 0

    lax.fori_loop(0, 7, pass_done, 0)
    remote(zfar.at[0], zfar.at[2], zf_s.at[0], zf_r.at[0], at_z(down)).wait_send()
    remote(zfar.at[1], zfar.at[3], zf_s.at[1], zf_r.at[1], at_z(up)).wait_send()
    sent(ag, ag_s, ag_r, me_r, at_r)

    sent(amp, rs_s, rs_r, me_r, at_r)
    sent(obuf, o_s, o_r, me_r, at_r)
    remote(cb.at[core], cb.at[core], cb_s.at[0], cb_r.at[0], sibling).wait_send()

    def settle_quads(q, _):
        quad_ref = mine.at[pl.ds(4 * q, 4)]
        remote(quad_ref, quad_ref, fwd_s.at[q], fwd_r.at[q], sibling).wait_send()
        return 0

    lax.fori_loop(0, 4, settle_quads, 0)
    arrived(rbuf, o_s, o_r, me_r, at_r)
    total = jnp.sum(rbuf[...], axis=0)
    total = jnp.concatenate([total, pltpu.roll(total, 64, 1)], axis=0)[:, :64]
    field = permuted(total, unperm[...]) * (COUPLING * KAPPA)
    pr, pi = ipr[...], ipi[...]
    for d in range(2):
        for c in range(3):
            a, b = part[c]
            pre, pim = mom[d, c, 0:1], mom[d, c, 1:2]
            k = 6 * d + c
            mre = a[2 * d : 2 * d + 1] - b[2 * d + 1 : 2 * d + 2]
            mim = a[2 * d + 1 : 2 * d + 2] + b[2 * d : 2 * d + 1]
            out[d, c, 0:1] = pr * pre - pi * pim - field[k : k + 1, :64] - mre
            out[d, c, 1:2] = pr * pim + pi * pre - field[k + 3 : k + 4, :64] - mim


def on_device(positions, moments, inv_polar_re, inv_polar_im, mode_field, mode_detune, mode_width):
    table = perm_map()
    back = np.zeros((64, 128), np.float32)
    back[:, :64] = table[:, :64].T
    vm = pl.BlockSpec(memory_space=pltpu.VMEM)
    dma = lambda n: pltpu.SemaphoreType.DMA((n,))
    arrays = (
        positions,
        moments.transpose(0, 2, 1, 3),
        inv_polar_re.reshape(1, -1),
        inv_polar_im.reshape(1, -1),
        mode_field,
        mode_detune.reshape(1, -1),
        mode_width.reshape(1, -1),
        jnp.asarray(feature_maps(), BF16),
        jnp.asarray(table, BF16),
        jnp.asarray(back, BF16),
    )
    response = pl.pallas_call(
        kernel,
        out_shape=jax.ShapeDtypeStruct(arrays[1].shape, F32),
        in_specs=[pl.BlockSpec(memory_space=pl.ANY)] * 10,
        out_specs=vm,
        scratch_shapes=[pltpu.VMEM(a.shape, a.dtype) for a in arrays]
        + [
            dma(10),
            pltpu.VMEM((2, 16, 8, 128), F32),
            pltpu.VMEM((16, 8, 128), F32),
            pltpu.VMEM((4, 128, 256), BF16),
            pltpu.VMEM((4, 8, 256), F32),
            pltpu.VMEM((2, 4, 128, 1024), BF16),
            pltpu.VMEM((256, 128), BF16),
            pltpu.VMEM((2, 1024, 256), BF16),
            pltpu.VMEM((2, 1024, 256), BF16),
            pltpu.VMEM((256, 256), F32),
            pltpu.VMEM((256, 256), F32),
            pltpu.VMEM((2, 4, 128, 256), F32),
            pltpu.VMEM((16, 1, 128), F32),
            pltpu.VMEM((16, 1, 128), F32),
            pltpu.VMEM((16, 1, 128), F32),
            pltpu.VMEM((2, 1, 128), F32),
            pltpu.VMEM((16, 1, 128), F32),
            pltpu.VMEM((16, 8, 128), F32),
            pltpu.VMEM((16, 8, 128), F32),
        ]
        + [dma(16), dma(16), dma(16), dma(16), dma(4), dma(4), dma(16), dma(16)]
        + [dma(16), dma(16), dma(1), dma(1), dma(16), dma(16), dma(16), dma(16)]
        + [dma(7), dma(2), dma(2), pltpu.VMEM((5, 1, 128), F32)],
        compiler_params=pltpu.CompilerParams(collective_id=0, has_side_effects=True, vmem_limit_bytes=60 << 20),
    )(*arrays)
    return response.transpose(0, 2, 1, 3)


def solution(mesh):
    both = ("blk", "grp")
    placed = (P(None, both), P(None, None, None, both), P(both), P(both), P(None, None, both, None), P(), P())
    return jax.shard_map(on_device, mesh=mesh, in_specs=placed, out_specs=P(None, None, None, both), check_vma=False)
```

```python
import math

import jax
import jax.numpy as jnp
import numpy as np
from jax import lax
from jax.experimental import pallas as pl
from jax.experimental.pallas import tpu as pltpu
from jax.sharding import PartitionSpec as P

F32, BF16 = jnp.float32, jnp.bfloat16
MESH = pl.DeviceIdType.MESH
KAPPA = 1.0 / (2.0 * math.pi)
COUPLING = 0.05
SHIFT = 1.25
HUGE = 1e30


def feature_maps():
    e = np.zeros((4, 160, 96), np.float32)
    for c in range(4):
        delta = (c - 1.5) * SHIFT
        base = np.zeros((160, 32), np.float32)
        for d in range(2):
            for j in range(15):
                row = j * 2 + d
                if j < 3:
                    base[row, 3] = 1.0; comp = j
                elif j < 12:
                    a, comp = divmod(j - 3, 3)
                else:
                    a, comp = j - 12, None
                if j >= 3:
                    base[row, a] = 1.0
                    if a == 0: base[row, 3] = -delta
                for ri in range(2):
                    m = 4 + d * 6 + ri * 3
                    if comp is not None:
                        base[32 + 32 * ri + row, m + comp] = -3.0
                    else:
                        base[32 + 32 * ri + row, 16 + d * 2 + ri] = -3.0
                        base[32 + 32 * ri + row, m] = 3.0 * delta
                        base[96 + 32 * ri + row, m + a] = 1.0
        for piece in range(3):
            e[c, :, 32 * piece:32 * piece + 32] = base
    return e


def pieces(v):
    h = v.astype(BF16).astype(F32)
    rest = v - h
    m = rest.astype(BF16).astype(F32)
    return h, m, rest - m


S4 = [4.442867982147176, -7.307445408741119, 3.59480206222511, -0.7844035161415288]
C5 = [1.4142134965690698, -6.978850988398392, 5.73946117217025, -1.8835629909695983, 0.3106981907767927]

def planes(r2):
    y = lax.rsqrt(r2)
    w = r2 * y
    f = w - jnp.round(w)
    t = f * f
    s = S4[-1]
    for k in S4[-2::-1]: s = s * t + k
    s = s * f
    c = C5[-1]
    for k in C5[-2::-1]: c = c * t + k
    y23 = y * (2.0 / 3.0)
    sy = s * y23
    gr = y23 - s * sy
    gi = sy * c
    q = y * y
    u = y * (1.5 * KAPPA)
    v1 = 1.5 - q * (1.5 * KAPPA * KAPPA)
    ar = gr * v1 - gi * u
    ai = gi * v1 + gr * u
    br = q * (ar - gr)
    bi = q * (ai - gi)
    return ar, ai, br, bi


def split(v):
    h = v.astype(BF16)
    return h, (v - h.astype(F32)).astype(BF16)


def perm_map():
    m = np.zeros((64, 128), np.float32)
    for r in range(2):
        for c in range(4):
            for x in range(8):
                m[32 * r + 8 * c + x, 16 * c + 8 * r + x] = 1.0
    m[:, 64:] = m[:, :64]
    return m


def prep_targets(tpos, o_t, tag_dev, ta, xrow):
    lane8 = lax.broadcasted_iota(jnp.int32, (8, 128), 1)
    lane = lax.broadcasted_iota(jnp.int32, (8, 256), 1)
    sub = lax.broadcasted_iota(jnp.int32, (8, 256), 0)
    org = jnp.where(sub == 0, o_t[0], jnp.where(sub == 1, o_t[1], o_t[2]))
    jrow = lax.broadcasted_iota(jnp.int32, (64, 256), 0)
    jlane = lax.broadcasted_iota(jnp.int32, (64, 256), 1)
    for c in range(4):
        halves = []
        for t in range(2):
            v = jnp.zeros((8, 128), F32)
            for k in range(8):
                shift = (16 * (k - c)) % 128
                a = tpos[8 * t + k]
                if shift: a = pltpu.roll(a, shift, 1)
                v = jnp.where(lane8 // 16 == k, a, v)
            halves.append(v)
        raw = jnp.concatenate(halves, axis=1)
        delta = (c - 1.5) * SHIFT
        loc = (raw - org) * KAPPA - jnp.where(sub == 0, delta, 0.0)
        loc = jnp.where(sub < 3, loc, 0.0)
        xrow[c] = loc
        n2 = jnp.sum(loc * loc, axis=0, keepdims=True)
        v = jnp.where(sub == c, -2.0 * loc[0:1], jnp.where(sub == 4, -2.0 * loc[1:2], jnp.where(sub == 5, -2.0 * loc[2:3], jnp.where(sub == 6, n2, 0.0))))
        h, m, l = pieces(v)
        g6 = jnp.where((sub == c) | (sub == 4 + c), 1.0, 0.0)
        g7 = jnp.where(sub == c, 1.0, 0.0)
        tag = jnp.where((jlane // 16 == tag_dev) & (jrow == 16 * c + jlane % 16), HUGE, 0.0)
        ta[c] = jnp.concatenate([h, m, l, h, m, h, g6, g7, tag], axis=0).astype(BF16)


def prep_sources(src, slot, o_s, oy_r2, own_tag, emap, wmat, sb):
    low = lax.broadcasted_iota(jnp.int32, (8, 128), 1) < 64
    ra, rb = [], []
    for p in range(2):
        a, b = src[4 * slot + 2 * p], src[4 * slot + 2 * p + 1]
        ra.append(jnp.where(low, a, pltpu.roll(b, 64, 1)))
        rb.append(jnp.where(low, pltpu.roll(a, 64, 1), b))
    fa = jnp.concatenate(ra, axis=1)
    fb = jnp.concatenate(rb, axis=1)
    sub = lax.broadcasted_iota(jnp.int32, (8, 256), 0)
    org = jnp.where(sub == 0, o_s[0], jnp.where(sub == 1, o_s[1], o_s[2]))
    loc = (fa - org) * KAPPA
    yr2 = (fa[1:2] - oy_r2) * KAPPA
    f0 = jnp.where(sub < 3, loc, jnp.where(sub == 3, 1.0, fa))
    xs = [f0[k:k + 1] for k in range(3)]
    mom = [f0[4 + k:5 + k] for k in range(4)] + [fb[k:k + 1] for k in range(8)]
    us = []
    for d in range(2):
        for ri in range(2):
            b = d * 6 + ri * 3
            us.append(xs[0] * mom[b] + xs[1] * mom[b + 1] + xs[2] * mom[b + 2])
    f2 = jnp.concatenate(us + [jnp.zeros((4, 256), F32)], axis=0)
    feats = jnp.concatenate([f0, fb, f2, jnp.zeros((8, 256), F32)], axis=0)
    h, m, l = pieces(feats)
    frp = jnp.concatenate([h, m, l], axis=0).astype(BF16)
    for c in range(4):
        o = jnp.dot(emap[c], frp, preferred_element_type=F32)
        xe = o[:32]
        pr, pi = o[32:64] * xe, o[64:96] * xe
        ar, ai = o[96:128], o[128:160]
        for k, (re, im) in enumerate(((ar, ai), (pr, pi))):
            rh, rl = split(re); ih, il = split(im)
            wmat[c, :, pl.ds(512 * k, 256)] = jnp.concatenate([rh, ih, rl, il], axis=0)
            wmat[c, :, pl.ds(512 * k + 256, 256)] = jnp.concatenate([-ih, rh, -il, rl], axis=0)
    lane = lax.broadcasted_iota(jnp.int32, (64, 256), 1)
    j = lax.broadcasted_iota(jnp.int32, (64, 256), 0)
    tag = jnp.where(lane == own_tag + j, 1.0, 0.0)
    shift = (sub.astype(F32) - 1.5) * SHIFT
    va = jnp.where(sub < 4, xs[0] - shift, jnp.where(sub == 4, yr2, jnp.where(sub == 5, xs[2], jnp.where(sub == 6, 1.0, 0.0))))
    yz = yr2 * yr2 + xs[2] * xs[2]
    vb = jnp.where(sub < 4, va * va + yz, 0.0)
    ah, am, al = pieces(va); bh, bm, bl = pieces(vb)
    b6 = jnp.where(sub < 4, bh, pltpu.roll(bm, 4, 0))
    rows = jnp.concatenate([ah, ah, ah, am, am, al, b6, bl, tag], axis=0)
    sb[...] = jnp.concatenate([rows[:, :128].T, rows[:, 128:].T], axis=0).astype(BF16)


def finish(acc, xr, dy):
    t = acc[:64] + acc[64:]
    x = [xr[k:k + 1] for k in range(3)]
    x[1] = x[1] + dy
    out = [None] * 12
    for ri in range(2):
        row = lambda j: t[ri * 32 + 2 * j:ri * 32 + 2 * j + 2]
        s1 = [row(k) for k in range(3)]
        s2 = [[row(3 + 3 * a + k) for k in range(3)] for a in range(3)]
        s3 = [row(12 + k) for k in range(3)]
        inner = x[0] * s1[0] + x[1] * s1[1] + x[2] * s1[2] - (s2[0][0] + s2[1][1] + s2[2][2])
        for c in range(3):
            val = s3[c] + x[c] * inner - (x[0] * s2[c][0] + x[1] * s2[c][1] + x[2] * s2[c][2])
            for d in range(2):
                out[d * 6 + ri * 3 + c] = val[d:d + 1]
    return jnp.concatenate(out, axis=0)


def nn(a, b):
    return lax.dot_general(a, b, (((1,), (0,)), ((), ())), precision=lax.Precision.HIGHEST, preferred_element_type=F32)


def nt(a, b):
    return lax.dot_general(a, b, (((1,), (1,)), ((), ())), precision=lax.Precision.HIGHEST, preferred_element_type=F32)


def permuted(rows, table):
    h, m, l = pieces(rows)
    n = rows.shape[0]
    o = jnp.dot(jnp.concatenate([h, m, l], axis=0).astype(BF16), table, preferred_element_type=F32)
    return o[:n] + o[n : 2 * n] + o[2 * n :]


def kernel(pos_h, mom_h, ipr_h, ipi_h, mode_h, det_h, wid_h, emap_h, perm_h, unperm_h, out,
           pos, mom, ipr, ipi, mode, det, wid, emap, perm, unperm, in_sem,
           src, tgt, ta, xrow, wmat, sb, ga, gb, ra, rb, acc, amp, rs, zb, cb, ag, obuf, rbuf,
           tgt_s, tgt_r, src_s, src_r, fwd_s, fwd_r, rs_s, rs_r, zb_s, zb_r, cb_s, cb_r, ag_s, ag_r, o_s, o_r, pass_s, zf_s, zf_r, zfar):
    blk, grp = lax.axis_index("blk"), lax.axis_index("grp")
    zl, x, zh, y, core = blk // 4, blk % 4, grp // 8, (grp // 2) % 4, grp % 2
    me_r, me_z = x * 4 + y, zh * 8 + zl

    def at_r(r):
        return (zl * 4 + r // 4, zh * 8 + (r % 4) * 2 + core)

    def at_z(z):
        return ((z % 8) * 4 + x, (z // 8) * 8 + y * 2 + core)

    sibling = (blk, zh * 8 + y * 2 + (1 - core))

    fetched = [
        pltpu.make_async_copy(a, b, in_sem.at[k])
        for k, (a, b) in enumerate(
            zip(
                (pos_h, mom_h, perm_h, mode_h, emap_h, det_h, wid_h, ipr_h, ipi_h, unperm_h),
                (pos, mom, perm, mode, emap, det, wid, ipr, ipi, unperm),
            )
        )
    ]
    for copy in fetched:
        copy.start()

    barrier = pltpu.get_barrier_semaphore()

    def greet(s, _):
        pl.semaphore_signal(barrier, inc=1, device_id=at_r((me_r + s) % 16), device_id_type=MESH)
        return 0

    def greet_z(s, _):
        pl.semaphore_signal(barrier, inc=1, device_id=at_z(near(s)), device_id_type=MESH)
        return 0

    def near(s):
        return (me_z + 12 + s + s // 4) % 16

    lax.fori_loop(0, 8, greet_z, 0, unroll=4)
    lax.fori_loop(1, 16, greet, 0, unroll=5)
    pl.semaphore_signal(barrier, inc=1, device_id=sibling, device_id_type=MESH)


    mine = src.at[core]

    def remote(a, b, ss, rr, dev):
        return pltpu.make_async_remote_copy(src_ref=a, dst_ref=b, send_sem=ss, recv_sem=rr, device_id=dev, device_id_type=MESH)

    def spread_to(buf, ss, rr, me, where):
        def go(s, _):
            j = (me + s) % 16
            remote(buf.at[me], buf.at[me], ss.at[0], rr.at[0], where(j)).start()
            return 0
        lax.fori_loop(1, 16, go, 0, unroll=5)

    def arrived(buf, ss, rr, me, where):
        many = buf.at[pl.ds(0, 15)]
        remote(many, many, ss.at[0], rr.at[0], where((me + 1) % 16)).wait_recv()

    def near_spread(buf, ss, rr):
        def go(s, _):
            z = near(s)
            remote(buf.at[me_z], buf.at[me_z], ss.at[z], rr.at[me_z], at_z(z)).start()
            return 0
        lax.fori_loop(0, 8, go, 0, unroll=4)

    def near_arrived(buf, ss, rr):
        def go(s, _):
            z = near(s)
            remote(buf.at[z], buf.at[z], ss.at[z], rr.at[z], at_z(z)).wait_recv()
            return 0
        lax.fori_loop(0, 8, go, 0)

    def near_sent(buf, ss, rr):
        def go(s, _):
            z = near(s)
            remote(buf.at[me_z], buf.at[me_z], ss.at[z], rr.at[me_z], at_z(z)).wait_send()
            return 0
        lax.fori_loop(0, 8, go, 0)

    up, down = (me_z + 4) % 16, (me_z + 12) % 16

    def passed(k):
        z = (me_z + jnp.where(k < 4, k + 1, 19 - k)) % 16
        to = jnp.where(k < 4, down, up)
        return remote(mine.at[z], mine.at[z], pass_s.at[k], src_r.at[z], at_z(to))

    def sent(buf, ss, rr, me, where):
        many = buf.at[pl.ds(0, 15)]
        remote(many, many, ss.at[0], rr.at[0], where((me + 1) % 16)).wait_send()

    for copy in fetched[:3]:
        copy.wait()
    feats = jnp.concatenate(
        [pos[...], jnp.ones((1, 64), F32)]
        + [mom[d, c, ri : ri + 1] for d in range(2) for ri in range(2) for c in range(3)],
        axis=0,
    )
    moved = permuted(feats, perm[...])
    low = lax.broadcasted_iota(jnp.int32, (8, 128), 1) < 64
    tile = jnp.where(low, moved[:8], moved[8:])
    src[core, me_z] = tile
    tgt[me_r] = tile

    acc[...] = jnp.zeros_like(acc)
    gb[...] = jnp.zeros_like(gb)
    wmat[1, 3] = jnp.zeros((128, 1024), BF16)
    pl.semaphore_wait(barrier, 24)

    spread_to(tgt, tgt_s, tgt_r, me_r, at_r)
    near_spread(mine, src_s, src_r)

    fetched[3].wait()
    pa, pb = 0.0, 0.0
    for c in range(3):
        pc = jnp.concatenate([mom[d, c] for d in range(2)], axis=0)
        pa = pa + nn(pc, mode[0, c])
        pb = pb + nn(pc, mode[1, c])
    for d in range(2):
        re = pa[2 * d : 2 * d + 1] - pb[2 * d + 1 : 2 * d + 2]
        im = pa[2 * d + 1 : 2 * d + 2] + pb[2 * d : 2 * d + 1]
        for q in range(4):
            amp[8 * d + q] = re[:, 128 * q : 128 * q + 128]
            amp[8 * d + 4 + q] = im[:, 128 * q : 128 * q + 128]
    for copy in fetched[4:]:
        copy.wait()

    def scatter(s, _):
        j = (me_r + s) % 16
        remote(amp.at[j], rs.at[me_r], rs_s.at[0], rs_r.at[0], at_r(j)).start()
        return 0

    lax.fori_loop(1, 16, scatter, 0, unroll=5)
    rs[me_r] = amp[me_r]

    ox, oz, oyt = 15.5, 4.0 * zl.astype(F32) + 1.5, (16 * zh + 2 * core).astype(F32) + 6.5
    near_arrived(mine, src_s, src_r)

    def pass_on(k, _):
        passed(k).start()
        return 0

    lax.fori_loop(0, 7, pass_on, 0, unroll=7)
    arrived(tgt, tgt_s, tgt_r, me_r, at_r)
    prep_targets(tgt, (ox, oyt, oz), me_r, ta, xrow)

    def stage(w, gold, gnew, rnow, nxt, rnext):
        total = None
        for q in range(8):
            ko = 256 * (q % 4)
            part = jnp.dot(w[:, ko : ko + 256], gold[q // 4, ko : ko + 256], preferred_element_type=F32)
            if nxt is not None and q % 4 == 0:
                top = 32 * q
                r2 = jnp.dot(sb[top : top + 128], ta[nxt], preferred_element_type=F32)
            for k in (2 * q, 2 * q + 1):
                for n, v in enumerate(planes(rnow[16 * k : 16 * k + 16, :])):
                    h, l = split(v)
                    gnew[0, 256 * n + 16 * k : 256 * n + 16 * k + 16, :] = h
                    gnew[1, 256 * n + 16 * k : 256 * n + 16 * k + 16, :] = l
            if nxt is not None and q % 4 == 0:
                rnext[top : top + 128] = r2
            total = part if total is None else total + part
        return total

    def one_block(step, _):
        quad = (me_z // 4 + step // 2) % 4
        away = step % 2
        from_core = (core + away) % 2
        quad_ref = src.at[from_core, pl.ds(4 * quad, 4)]

        @pl.when(away == 0)
        def _():
            def go(k, _):
                z = 4 * quad + k
                gap = (z + 20 - me_z) % 16
                @pl.when(gap > 8)
                def _():
                    remote(mine.at[z], mine.at[z], src_s.at[z], src_r.at[z], at_z(z)).wait_recv()
                return 0
            lax.fori_loop(0, 4, go, 0)
            remote(quad_ref, quad_ref, fwd_s.at[quad], fwd_r.at[quad], sibling).start()

        @pl.when(away == 1)
        def _():
            remote(quad_ref, quad_ref, fwd_s.at[quad], fwd_r.at[quad], sibling).wait_recv()

        half = quad // 2
        oys = (16 * half + 4 * y).astype(F32) + 1.5
        own = jnp.where(step == 0, (me_z % 4) * 64, -1000)
        par = step % 2
        prep_sources(src.at[from_core], quad, (ox, oys, oz), oyt, own, emap, wmat.at[par], sb)
        ra[...] = jnp.dot(sb[...], ta[0], preferred_element_type=F32)
        before = ((me_z // 4 + (step + 7) // 2) % 4) // 2
        acc[before, 3] += stage(wmat.at[1 - par, 3], gb, ga, ra, 1, rb)
        acc[half, 0] += stage(wmat.at[par, 0], ga, gb, rb, 2, ra)
        acc[half, 1] += stage(wmat.at[par, 1], gb, ga, ra, 3, rb)
        acc[half, 2] += stage(wmat.at[par, 2], ga, gb, rb, None, None)

        @pl.when(step == 1)
        def _():
            arrived(rs, rs_s, rs_r, me_r, at_r)
            zb[me_z] = jnp.sum(rs[...], axis=0)
            near_spread(zb, zb_s, zb_r)

        @pl.when(step == 3)
        def _():
            near_arrived(zb, zb_s, zb_r)
            above = zb[(me_z + 1) % 16] + zb[(me_z + 2) % 16] + zb[(me_z + 3) % 16]
            above = above + zb[up]
            below = zb[(me_z + 15) % 16] + zb[(me_z + 14) % 16] + zb[(me_z + 13) % 16]
            zfar[0] = above
            zfar[1] = below
            zfar[4] = above + below + zb[down] + zb[me_z]
            remote(zfar.at[0], zfar.at[2], zf_s.at[0], zf_r.at[0], at_z(down)).start()
            remote(zfar.at[1], zfar.at[3], zf_s.at[1], zf_r.at[1], at_z(up)).start()

        @pl.when(step == 5)
        def _():
            remote(zfar.at[0], zfar.at[2], zf_s.at[0], zf_r.at[0], at_z(up)).wait_recv()
            remote(zfar.at[1], zfar.at[3], zf_s.at[1], zf_r.at[1], at_z(down)).wait_recv()
            cb[core] = zfar[2] + zfar[3] + zfar[4]
            remote(cb.at[core], cb.at[core], cb_s.at[0], cb_r.at[0], sibling).start()

        @pl.when(step == 6)
        def _():
            remote(cb.at[1 - core], cb.at[1 - core], cb_s.at[0], cb_r.at[0], sibling).wait_recv()
            ag[me_r] = cb[0] + cb[1]
            spread_to(ag, ag_s, ag_r, me_r, at_r)

        return 0

    lax.fori_loop(0, 8, one_block, 0)
    last = ((me_z // 4 + 3) % 4) // 2
    w = wmat[1, 3]
    acc[last, 3] += jnp.dot(w, gb[0], preferred_element_type=F32) + jnp.dot(w, gb[1], preferred_element_type=F32)

    lane = lax.broadcasted_iota(jnp.int32, (8, 128), 1)
    fa, fb = [], []
    for c in range(4):
        f = 0.0
        for half in range(2):
            dy = (oyt - ((16 * half + 4 * y).astype(F32) + 1.5)) * KAPPA
            f = f + finish(acc[half, c], xrow[c], dy)
        fa.append(f[:8])
        fb.append(jnp.concatenate([f[8:], jnp.zeros((4, 256), F32)], axis=0))
    for r in range(16):
        t, k = r // 8, r % 8
        v = jnp.zeros((8, 128), F32)
        for c in range(4):
            for top, rows in ((0, fa[c]), (64, fb[c])):
                a = rows[:, 128 * t : 128 * t + 128]
                shift = (top + 16 * (c - k)) % 128
                if shift:
                    a = pltpu.roll(a, shift, 1)
                v = jnp.where(lane // 16 == top // 16 + c, a, v)
        obuf[r] = v

    def give(s, _):
        j = (me_r + s) % 16
        remote(obuf.at[j], rbuf.at[me_r], o_s.at[0], o_r.at[0], at_r(j)).start()
        return 0

    lax.fori_loop(1, 16, give, 0, unroll=5)
    rbuf[me_r] = obuf[me_r]

    arrived(ag, ag_s, ag_r, me_r, at_r)
    rows = [jnp.concatenate([ag[4 * k + q] for q in range(4)], axis=1) for k in range(4)]
    den = det[...] * det[...] + wid[...] * wid[...]
    rr, ri = det[...] / den, wid[...] / den
    weighted = []
    for d in range(2):
        re, im = rows[2 * d], rows[2 * d + 1]
        weighted += [rr * re - ri * im, rr * im + ri * re]
    weighted = jnp.concatenate(weighted, axis=0)
    part = []
    for c in range(3):
        part.append((nt(weighted, mode[0, c]), nt(weighted, mode[1, c])))

    sent(tgt, tgt_s, tgt_r, me_r, at_r)
    near_sent(mine, src_s, src_r)
    near_sent(zb, zb_s, zb_r)

    def pass_done(k, _):
        passed(k).wait_send()
        return 0

    lax.fori_loop(0, 7, pass_done, 0)
    remote(zfar.at[0], zfar.at[2], zf_s.at[0], zf_r.at[0], at_z(down)).wait_send()
    remote(zfar.at[1], zfar.at[3], zf_s.at[1], zf_r.at[1], at_z(up)).wait_send()
    sent(ag, ag_s, ag_r, me_r, at_r)

    sent(amp, rs_s, rs_r, me_r, at_r)
    sent(obuf, o_s, o_r, me_r, at_r)
    remote(cb.at[core], cb.at[core], cb_s.at[0], cb_r.at[0], sibling).wait_send()

    def settle_quads(q, _):
        quad_ref = mine.at[pl.ds(4 * q, 4)]
        remote(quad_ref, quad_ref, fwd_s.at[q], fwd_r.at[q], sibling).wait_send()
        return 0

    lax.fori_loop(0, 4, settle_quads, 0)
    arrived(rbuf, o_s, o_r, me_r, at_r)
    total = jnp.sum(rbuf[...], axis=0)
    total = jnp.concatenate([total, pltpu.roll(total, 64, 1)], axis=0)[:, :64]
    field = permuted(total, unperm[...]) * (COUPLING * KAPPA)
    pr, pi = ipr[...], ipi[...]
    for d in range(2):
        for c in range(3):
            a, b = part[c]
            pre, pim = mom[d, c, 0:1], mom[d, c, 1:2]
            k = 6 * d + c
            mre = a[2 * d : 2 * d + 1] - b[2 * d + 1 : 2 * d + 2]
            mim = a[2 * d + 1 : 2 * d + 2] + b[2 * d : 2 * d + 1]
            out[d, c, 0:1] = pr * pre - pi * pim - field[k : k + 1, :64] - mre
            out[d, c, 1:2] = pr * pim + pi * pre - field[k + 3 : k + 4, :64] - mim


def on_device(positions, moments, inv_polar_re, inv_polar_im, mode_field, mode_detune, mode_width):
    table = perm_map()
    back = np.zeros((64, 128), np.float32)
    back[:, :64] = table[:, :64].T
    vm = pl.BlockSpec(memory_space=pltpu.VMEM)
    dma = lambda n: pltpu.SemaphoreType.DMA((n,))
    arrays = (
        positions,
        moments.transpose(0, 2, 1, 3),
        inv_polar_re.reshape(1, -1),
        inv_polar_im.reshape(1, -1),
        mode_field,
        mode_detune.reshape(1, -1),
        mode_width.reshape(1, -1),
        jnp.asarray(feature_maps(), BF16),
        jnp.asarray(table, BF16),
        jnp.asarray(back, BF16),
    )
    response = pl.pallas_call(
        kernel,
        out_shape=jax.ShapeDtypeStruct(arrays[1].shape, F32),
        in_specs=[pl.BlockSpec(memory_space=pl.ANY)] * 10,
        out_specs=vm,
        scratch_shapes=[pltpu.VMEM(a.shape, a.dtype) for a in arrays]
        + [
            dma(10),
            pltpu.VMEM((2, 16, 8, 128), F32),
            pltpu.VMEM((16, 8, 128), F32),
            pltpu.VMEM((4, 128, 256), BF16),
            pltpu.VMEM((4, 8, 256), F32),
            pltpu.VMEM((2, 4, 128, 1024), BF16),
            pltpu.VMEM((256, 128), BF16),
            pltpu.VMEM((2, 1024, 256), BF16),
            pltpu.VMEM((2, 1024, 256), BF16),
            pltpu.VMEM((256, 256), F32),
            pltpu.VMEM((256, 256), F32),
            pltpu.VMEM((2, 4, 128, 256), F32),
            pltpu.VMEM((16, 1, 128), F32),
            pltpu.VMEM((16, 1, 128), F32),
            pltpu.VMEM((16, 1, 128), F32),
            pltpu.VMEM((2, 1, 128), F32),
            pltpu.VMEM((16, 1, 128), F32),
            pltpu.VMEM((16, 8, 128), F32),
            pltpu.VMEM((16, 8, 128), F32),
        ]
        + [dma(16), dma(16), dma(16), dma(16), dma(4), dma(4), dma(16), dma(16)]
        + [dma(16), dma(16), dma(1), dma(1), dma(16), dma(16), dma(16), dma(16)]
        + [dma(7), dma(2), dma(2), pltpu.VMEM((5, 1, 128), F32)],
        compiler_params=pltpu.CompilerParams(collective_id=0, has_side_effects=True, vmem_limit_bytes=60 << 20),
    )(*arrays)
    return response.transpose(0, 2, 1, 3)


def solution(mesh):
    both = ("blk", "grp")
    placed = (P(None, both), P(None, None, None, both), P(both), P(both), P(None, None, both, None), P(), P())
    return jax.shard_map(on_device, mesh=mesh, in_specs=placed, out_specs=P(None, None, None, both), check_vma=False)
```
